256 devices in a mesh: row: 8 (over x, z_hi), samp: 32 (over y, z_lo, core).
Axes of the slice: x: 4, y: 4, z: 8 (z_hi: 2, z_lo: 4; z = z_hi * 4 + z_lo), core: 2. Of those that a mesh axis runs over, the one named last changes fastest.
Arguments:
- activations: bfloat16 [32, 1024, 768], P('samp', 'row'), may hold values from -6 to 6
- pair_bias: bfloat16 [16, 1024, 1024], P(None, ('row', 'samp')), may hold values from -10 to 240
- w_qkv: bfloat16 [768, 2304], replicated, may hold values from -0.21875 to 0.21875
- w_out: bfloat16 [768, 768], replicated, may hold values from -0.21875 to 0.21875
- cotangent: bfloat16 [32, 1024, 768], P('samp', 'row'), may hold values from -6 to 6
Outputs:
- update: bfloat16 [32, 1024, 768], P('samp', 'row')
- grad_act: bfloat16 [32, 1024, 768], P('samp', 'row')
- grad_pair: bfloat16 [16, 1024, 1024], P(None, ('row', 'samp'))
- grad_weights: float32 [768, 3072], P(('row', 'samp'))
The draws below stay inside these ranges and needn't reach their ends.
All inputs are finite; a program needn't handle non-finite values.
Results may differ from the reference program's by a relative error of at most 0.025.
Values may be sent and summed in bfloat16 or wider, within the bound.
No kernel may reach another device: no remote copies, remote signals or barrier semaphores. Data moves between devices by JAX's collectives and lax.ppermute only.
A program may use at most 128 MiB of HBM per device.

```python
import math
import jax
import jax.numpy as jnp
from jax import lax

D = 768
H = 16
N = 1024
SAMPLES = 32


def draw_pair_bias(key, part):
    key = jax.random.fold_in(key, 7)
    subkeys = jax.random.split(key, 1)
    values = jnp.clip(jax.random.normal(subkeys[0], (N, N, H), jnp.float32) * 3.0, -10.0, 10.0)
    return jnp.transpose(values, (2, 0, 1)).astype(jnp.bfloat16)


def level_of(stream_key, extent, shards, low, high):
    def one(axis_at, blocks):
        heights = jax.random.uniform(jax.random.fold_in(jax.random.fold_in(stream_key, 6), axis_at), (blocks,), jnp.float32, low / len(shards), high / len(shards))
        return jnp.repeat(jnp.exp(heights), extent[axis_at] // blocks).reshape((-1,) + (1,) * (len(extent) - axis_at - 1))

    factor_of = one(*shards[0])
    for cut in shards[1:]:
        factor_of = factor_of * one(*cut)
    return factor_of


def bell_draw(stream_key, shape, scale, most, pieces=(), dtype=jnp.bfloat16):
    values = scale * jax.random.normal(stream_key, shape, jnp.float32)
    if pieces:
        values = values * level_of(stream_key, shape, pieces, -0.22, 0.18)
    return jnp.clip(values, -most, most).astype(dtype)


def setup_inputs(seed: int = 0) -> dict:
    arg_keys = jax.random.split(jax.random.key(seed), 6)
    activations = bell_draw(arg_keys[0], (SAMPLES, N, D), 1.0, 6.0, ((0, 32), (1, 8)))
    pair_bias = draw_pair_bias(jax.random.fold_in(arg_keys[5], 71), 0)
    w_qkv = bell_draw(arg_keys[2], (D, 3 * D), D ** -0.5, 0.21875)
    w_out = bell_draw(arg_keys[3], (D, D), D ** -0.5, 0.21875)
    cotangent = bell_draw(arg_keys[4], (SAMPLES, N, D), 1.0, 6.0, ((0, 32), (1, 8)))
    return dict(activations=activations, pair_bias=pair_bias, w_qkv=w_qkv, w_out=w_out, cotangent=cotangent)


epsilon = 1e-05

def layer_norm(values):
    mean_value = lax.optimization_barrier(jnp.mean(values, axis=-1, keepdims=True))
    centred = values - mean_value
    variance = lax.optimization_barrier(jnp.mean(centred * centred, axis=-1, keepdims=True))
    inverse = lax.rsqrt(variance + epsilon)
    return (centred * inverse, inverse)

def norm_backward(grad_in, normed, inverse):
    first_mean = lax.optimization_barrier(jnp.mean(grad_in, axis=-1, keepdims=True))
    second_mean = lax.optimization_barrier(jnp.mean(grad_in * normed, axis=-1, keepdims=True))
    return inverse * (grad_in - first_mean - normed * second_mean)

def reference(activations, pair_bias, w_qkv, w_out, cotangent):
    head_size = D // H
    scale = 1.0 / math.sqrt(head_size)
    bias_heads = pair_bias.astype(jnp.float32)

    def one_sample(carry, inputs):
        pair_total, weight_total = carry
        sample_act, sample_cot = inputs
        normed, inverse = layer_norm(sample_act.astype(jnp.float32))
        normed_b = normed.astype(jnp.bfloat16)
        projected = jnp.dot(normed_b, w_qkv, preferred_element_type=jnp.float32).astype(jnp.bfloat16)
        queries = projected[:, :D].reshape(N, H, head_size).astype(jnp.float32)
        key_heads = projected[:, D:2 * D].reshape(N, H, head_size).astype(jnp.float32)
        value_heads = projected[:, 2 * D:].reshape(N, H, head_size).astype(jnp.float32)
        scores = jnp.einsum('qhd,khd->hqk', queries, key_heads) * scale + bias_heads
        peak = lax.optimization_barrier(jnp.max(scores, axis=-1, keepdims=True))
        expo = jnp.exp(scores - peak)
        probs = expo / lax.optimization_barrier(jnp.sum(expo, axis=-1, keepdims=True))
        probs_b = probs.astype(jnp.bfloat16)
        prob_f = probs_b.astype(jnp.float32)
        attended = jnp.einsum('hqk,khd->qhd', prob_f, value_heads).reshape(N, D).astype(jnp.bfloat16)
        update = jnp.dot(attended, w_out, preferred_element_type=jnp.float32).astype(jnp.bfloat16)
        grad_att = jnp.dot(sample_cot, w_out.T, preferred_element_type=jnp.float32).astype(jnp.bfloat16)
        grad_heads = grad_att.reshape(N, H, head_size).astype(jnp.float32)
        grad_prob = jnp.einsum('qhd,khd->hqk', grad_heads, value_heads)
        centre = lax.optimization_barrier(jnp.sum(probs * grad_prob, axis=-1, keepdims=True))
        grad_score = (probs * (grad_prob - centre)).astype(jnp.bfloat16)
        score_f = grad_score.astype(jnp.float32)
        grad_query = jnp.einsum('hqk,khd->qhd', score_f, key_heads).reshape(N, D) * scale
        grad_key = jnp.einsum('hqk,qhd->khd', score_f, queries).reshape(N, D) * scale
        grad_value = jnp.einsum('hqk,qhd->khd', prob_f, grad_heads).reshape(N, D)
        grad_qkv = jnp.concatenate([grad_query, grad_key, grad_value], axis=1).astype(jnp.bfloat16)
        grad_normed = jnp.dot(grad_qkv, w_qkv.T, preferred_element_type=jnp.float32)
        grad_act = norm_backward(grad_normed, normed, inverse).astype(jnp.bfloat16)
        weight_term = jnp.concatenate([jnp.dot(normed_b.T, grad_qkv, preferred_element_type=jnp.float32), jnp.dot(attended.T, sample_cot, preferred_element_type=jnp.float32)], axis=1)
        pair_total = pair_total + score_f
        return ((pair_total, weight_total + weight_term), (update, grad_act))
    start_carry = (jnp.zeros((H, N, N), jnp.float32), jnp.zeros((D, 4 * D), jnp.float32))
    (pair_total, weight_total), (updates, grads) = lax.scan(one_sample, start_carry, (activations, cotangent))
    return (updates, grads, pair_total.astype(jnp.bfloat16), weight_total)
```

```python
import math

import jax
import jax.numpy as jnp
from jax import lax
from jax.experimental import pallas as pl
from jax.experimental.pallas import tpu as pltpu
from jax.sharding import Mesh, PartitionSpec as P

H = 16
HEAD = 48
PAD = 128
AXES = ("x", "zh", "y", "zl", "c")

epsilon = 1e-05
F32 = jnp.float32
BF16 = jnp.bfloat16


def layer_norm(values):
    mean_value = jnp.mean(values, axis=-1, keepdims=True)
    centred = values - mean_value
    variance = jnp.mean(centred * centred, axis=-1, keepdims=True)
    inverse = lax.rsqrt(variance + epsilon)
    return (centred * inverse, inverse)


def norm_backward(grad_in, normed, inverse):
    first_mean = jnp.mean(grad_in, axis=-1, keepdims=True)
    second_mean = jnp.mean(grad_in * normed, axis=-1, keepdims=True)
    return inverse * (grad_in - first_mean - normed * second_mean)


def right_transposed(left, right):
    return lax.dot_general(left, right, (((1,), (1,)), ((), ())), preferred_element_type=F32)


def attention_kernel(scale, q_ref, k_ref, v_ref, g_ref, bias_ref, att_ref, dq_ref, dk_ref, dv_ref, pair_ref, dk_acc, dv_acc):
    block = pl.program_id(1)
    samples = q_ref.shape[0]

    @pl.when(block == 0)
    def _():
        dk_acc[...] = jnp.zeros_like(dk_acc)
        dv_acc[...] = jnp.zeros_like(dv_acc)

    pair = None
    for s in range(samples):
        q, k, v, g = q_ref[s], k_ref[s], v_ref[s], g_ref[s]
        scores = right_transposed(q, k) * scale + bias_ref[0].astype(F32)
        peak = jnp.max(scores, axis=-1, keepdims=True)
        expo = jnp.exp(scores - peak)
        probs = expo * (1.0 / jnp.sum(expo, axis=-1, keepdims=True))
        probs_b = probs.astype(BF16)
        att_ref[s] = jnp.dot(probs_b, v, preferred_element_type=F32).astype(BF16)
        grad_prob = right_transposed(g, v)
        centre = jnp.sum(probs * grad_prob, axis=-1, keepdims=True)
        grad_score = probs * (grad_prob - centre)
        score_b = grad_score.astype(BF16)
        pair = grad_score if pair is None else pair + grad_score
        dq_ref[s] = (jnp.dot(score_b, k, preferred_element_type=F32) * scale).astype(BF16)
        dk_acc[s] += jnp.dot(q.T, score_b, preferred_element_type=F32)
        dv_acc[s] += jnp.dot(g.T, probs_b, preferred_element_type=F32)
    pair_ref[0] = pair.astype(BF16)

    @pl.when(block == pl.num_programs(1) - 1)
    def _():
        for s in range(samples):
            dk_ref[s] = (dk_acc[s] * scale).astype(BF16)
            dv_ref[s] = dv_acc[s].astype(BF16)


def attention(queries, keys_values, grad_att, bias, scale):
    samples, rows, _ = queries.shape
    total = keys_values.shape[1]
    heads = bias.shape[0]
    step = 256
    q_spec = pl.BlockSpec((samples, step, PAD), lambda h, i: (0, i, h))
    kv_out = pl.BlockSpec((samples, PAD, total), lambda h, i: (0, h, 0))
    pair_spec = pl.BlockSpec((1, step, total), lambda h, i: (h, i, 0))
    return pl.pallas_call(
        lambda *refs: attention_kernel(scale, *refs),
        grid=(heads, rows // step),
        in_specs=[
            q_spec,
            pl.BlockSpec((samples, total, PAD), lambda h, i: (0, 0, h)),
            pl.BlockSpec((samples, total, PAD), lambda h, i: (0, 0, heads + h)),
            q_spec,
            pair_spec,
        ],
        out_specs=[q_spec, q_spec, kv_out, kv_out, pair_spec],
        out_shape=[
            jax.ShapeDtypeStruct(queries.shape, BF16),
            jax.ShapeDtypeStruct(queries.shape, BF16),
            jax.ShapeDtypeStruct((samples, heads * PAD, total), BF16),
            jax.ShapeDtypeStruct((samples, heads * PAD, total), BF16),
            jax.ShapeDtypeStruct(bias.shape, BF16),
        ],
        scratch_shapes=[pltpu.VMEM((samples, PAD, total), F32), pltpu.VMEM((samples, PAD, total), F32)],
        compiler_params=pltpu.CompilerParams(vmem_limit_bytes=48 * 1024 * 1024),
    )(queries, keys_values, keys_values, grad_att, bias)


def exchange(values, axes):
    return lax.all_to_all(values, axes, split_axis=0, concat_axis=0, tiled=True)


def ring(n, shift):
    return [(i, (i + shift) % n) for i in range(n)]


def pad_heads(columns):
    rows = columns.shape[0]
    heads = columns.shape[1] // HEAD
    padded = jnp.pad(columns.reshape(rows, heads, HEAD), ((0, 0), (0, 0), (0, PAD - HEAD)))
    return padded.reshape(rows, heads * PAD)


def drop_pad(values):
    lead = values.shape[:-1]
    heads = values.shape[-1] // PAD
    return values.reshape(*lead, heads, PAD)[..., :HEAD].reshape(*lead, heads * HEAD)


def ordered(flag, first, second):
    low = jnp.where(flag == 0, first, second)
    high = jnp.where(flag == 0, second, first)
    return low, high


def per_device(activations, pair_bias, w_qkv, w_out, cotangent):
    act = activations[0]
    cot = cotangent[0]
    rows, width = act.shape
    nx, nzh, ny, nzl, nc = (lax.axis_size(a) for a in AXES)
    at_x, at_zh, at_c = lax.axis_index("x"), lax.axis_index("zh"), lax.axis_index("c")
    groups = nx * nc
    heads = H // groups
    part = width // groups
    scale = 1.0 / math.sqrt(HEAD)
    total = pair_bias.shape[2]
    half = total // nzh
    own_rows = pair_bias.shape[1]
    swap = [(0, 1), (1, 0)]

    with jax.named_scope("bias_in"):
        send = pair_bias.reshape(nx, 1, 1, nc, heads, own_rows, total)
        send = jnp.broadcast_to(send, (nx, ny, nzl, nc, heads, own_rows, total))
        send = send.reshape(nx * ny * nzl * nc, heads, own_rows, total)
        bias = exchange(send, ("x", "y", "zl", "c"))
        bias = bias.transpose(1, 0, 2, 3).reshape(heads, half, total)

    with jax.named_scope("norm"):
        act_other = lax.ppermute(act, "zh", swap)
        normed, inverse = layer_norm(act.astype(F32))
        normed_b = normed.astype(BF16)
        other_b = layer_norm(act_other.astype(F32))[0].astype(BF16)
        low, high = ordered(at_zh, normed_b, other_b)
        pack = jnp.stack([low, high, cot])

    with jax.named_scope("gather"):
        from_low = lax.ppermute(pack, "x", ring(nx, 1))
        from_high = lax.ppermute(pack, "x", ring(nx, -1))
        relay = jnp.where(at_c == 0, from_low, from_high)
        pairs = []
        for i in range(nx):
            pairs.append((i * nc, ((i + 1) % nx) * nc))
            pairs.append((i * nc + 1, ((i - 1) % nx) * nc + 1))
        from_far = lax.ppermute(relay, ("x", "c"), pairs)
        full = jnp.zeros((nx,) + pack.shape, BF16)
        for shift, piece in ((0, pack), (1, from_high), (2, from_far), (3, from_low)):
            full = lax.dynamic_update_slice(full, piece[None], ((at_x + shift) % nx, 0, 0, 0))
        twin = lax.ppermute(full, "c", swap)
        both = jnp.stack([full, twin])
        normed_all = both[:, :, :nzh].reshape(2, total, width)
        normed_half = lax.dynamic_index_in_dim(both, at_zh, 2, keepdims=False).reshape(2, half, width)
        cot_half = both[:, :, nzh].reshape(2, half, width)

    with jax.named_scope("project"):
        group = at_x * nc + at_c
        own = [
            pad_heads(lax.dynamic_slice_in_dim(w_qkv, i * width + group * part, part, axis=1))
            for i in range(3)
        ]
        own_out = lax.dynamic_slice_in_dim(w_out, group * part, part, axis=0)
        own_out = jnp.pad(
            own_out.reshape(heads, HEAD, width), ((0, 0), (0, PAD - HEAD), (0, 0))
        ).reshape(heads * PAD, width)
        queries = jnp.dot(
            normed_half.reshape(2 * half, width), own[0], preferred_element_type=F32
        ).astype(BF16).reshape(2, half, heads * PAD)
        keys_values = jnp.dot(
            normed_all.reshape(2 * total, width),
            jnp.concatenate(own[1:], axis=1),
            preferred_element_type=F32,
        ).astype(BF16).reshape(2, total, 2 * heads * PAD)
        grad_att = right_transposed(
            cot_half.reshape(2 * half, width), own_out
        ).astype(BF16).reshape(2, half, heads * PAD)

    with jax.named_scope("attention"):
        att, dq, dk, dv, pair = attention(queries, keys_values, grad_att, bias, scale)

    with jax.named_scope("pair_out"):
        send = pair.reshape(heads, nx * ny * nzl * nc, own_rows, total).transpose(1, 0, 2, 3)
        got = exchange(send, ("x", "y", "zl", "c"))
        got = got.reshape(nx, ny, nzl, nc, heads, own_rows, total).astype(F32)
        grad_pair = jnp.sum(got, axis=(1, 2)).astype(BF16).reshape(H, own_rows, total)

    att = drop_pad(att)
    dq = drop_pad(dq)
    dk = dk.reshape(2, heads, PAD, total)[:, :, :HEAD].reshape(2, part, total)
    dv = dv.reshape(2, heads, PAD, total)[:, :, :HEAD].reshape(2, part, total)
    dkv = jnp.concatenate([dk, dv], axis=1)

    with jax.named_scope("tokens_out"):
        rowwise = jnp.concatenate([att, dq], axis=2).reshape(2, nx, rows, 2 * part)
        colwise = dkv.transpose(0, 2, 1).reshape(2, nx, nzh, rows, 2 * part)
        payload = jnp.concatenate([rowwise[:, :, None], colwise], axis=2)
        first, second = ordered(at_c, payload[0], payload[1])
        send = jnp.stack([first, second], axis=1).reshape(groups, (1 + nzh) * rows, 2 * part)
        got = exchange(send, ("x", "c")).reshape(groups, 1 + nzh, rows, 2, part)
        got = got.transpose(1, 2, 3, 0, 4).reshape(1 + nzh, rows, 2 * width)
        attended = got[0, :, :width]
        dkv_own = lax.dynamic_index_in_dim(got, 1 + at_zh, 0, keepdims=False)
        dkv_other = lax.dynamic_index_in_dim(got, 2 - at_zh, 0, keepdims=False)
        grad_other = right_transposed(dkv_other, w_qkv[:, width:]).astype(BF16)
        grad_other = lax.ppermute(grad_other, "zh", swap)
        update = jnp.dot(attended, w_out, preferred_element_type=F32).astype(BF16)
        grad_own = right_transposed(jnp.concatenate([got[0, :, width:], dkv_own], axis=1), w_qkv)
        grad_normed = grad_own + grad_other.astype(F32)
        grad_act = norm_backward(grad_normed, normed, inverse).astype(BF16)

    with jax.named_scope("weights_out"):
        weight_q = lax.dot_general(
            normed_half, dq, (((0, 1), (0, 1)), ((), ())), preferred_element_type=F32
        )
        weight_kv = lax.dot_general(
            normed_all, dkv, (((0, 1), (0, 2)), ((), ())), preferred_element_type=F32
        )
        weight_out = lax.dot_general(
            att, cot_half, (((0, 1), (0, 1)), ((), ())), preferred_element_type=F32
        )
        three = width // (nx * nzh * ny * nzl * nc)
        qkv_part = jnp.concatenate([weight_q, weight_kv], axis=1).astype(BF16)
        qkv_part = qkv_part.reshape(nx, nzh, ny, nzl, nc, three, 3 * part)
        qkv_part = qkv_part.transpose(2, 3, 0, 1, 4, 5, 6).reshape(ny * nzl, -1)
        out_part = weight_out.astype(BF16).reshape(ny * nzl, -1)
        cut = qkv_part.shape[1]
        got = exchange(jnp.concatenate([qkv_part, out_part], axis=1), ("y", "zl"))
        got = jnp.sum(got.astype(F32), axis=0).astype(BF16)
        qkv_part = got[:cut].reshape(nx, nzh, nc, three * 3 * part)
        out_part = got[cut:].reshape(1, 1, nc, three * width)
        here = (jnp.arange(nx) == at_x)[:, None] & (jnp.arange(nzh) == at_c)[None, :]
        out_part = jnp.where(here[:, :, None, None], out_part, jnp.zeros_like(out_part))
        send = jnp.concatenate([qkv_part, out_part], axis=3).reshape(nx * nzh * nc, -1)
        got = exchange(send, ("x", "zh", "c")).reshape(nx, nzh, nc, -1).astype(F32)
        qkv_part = jnp.sum(got[..., : three * 3 * part], axis=1)
        qkv_part = qkv_part.reshape(groups, three, 3, part).transpose(1, 2, 0, 3)
        out_part = jnp.sum(got[..., three * 3 * part :], axis=(0, 1, 2)).reshape(three, width)
        grad_weights = jnp.concatenate([qkv_part.reshape(three, 3 * width), out_part], axis=1)

    return (update[None], grad_act[None], grad_pair, grad_weights)


def solution(mesh):
    fine = Mesh(mesh.devices.reshape(4, 2, 4, 4, 2), AXES)
    row, samp = ("x", "zh"), ("y", "zl", "c")
    in_specs = (
        P(samp, row, None),
        P(None, row + samp, None),
        P(),
        P(),
        P(samp, row, None),
    )
    out_specs = (
        P(samp, row, None),
        P(samp, row, None),
        P(None, row + samp, None),
        P(row + samp, None),
    )
    return jax.shard_map(
        per_device, mesh=fine, in_specs=in_specs, out_specs=out_specs, check_vma=False
    )
```

```python
import math

import jax
import jax.numpy as jnp
from jax import lax
from jax.experimental import pallas as pl
from jax.experimental.pallas import tpu as pltpu
from jax.sharding import Mesh, PartitionSpec as P

H = 16
HEAD = 48
PAD = 128
AXES = ("x", "zh", "y", "zl", "c")
VMEM_LIMIT = 56 * 1024 * 1024

epsilon = 1e-05
F32 = jnp.float32
BF16 = jnp.bfloat16


def layer_norm(values):
    mean_value = jnp.mean(values, axis=-1, keepdims=True)
    centred = values - mean_value
    variance = jnp.mean(centred * centred, axis=-1, keepdims=True)
    inverse = lax.rsqrt(variance + epsilon)
    return (centred * inverse, inverse)


def norm_backward(grad_in, normed, inverse):
    first_mean = jnp.mean(grad_in, axis=-1, keepdims=True)
    second_mean = jnp.mean(grad_in * normed, axis=-1, keepdims=True)
    return inverse * (grad_in - first_mean - normed * second_mean)


def right_transposed(left, right):
    return lax.dot_general(left, right, (((1,), (1,)), ((), ())), preferred_element_type=F32)


def normalise(values):
    mean_value = jnp.mean(values, axis=-1, keepdims=True)
    centred = values - mean_value
    variance = jnp.mean(centred * centred, axis=-1, keepdims=True)
    return (centred * lax.rsqrt(variance + epsilon)).astype(BF16)


def cost(us):
    return pl.CostEstimate(flops=int(us * 1e9), bytes_accessed=int(us * 3e6), transcendentals=0)


def select_heads(window, offset):
    source = lax.broadcasted_iota(jnp.int32, (window.shape[1], 2 * PAD), 0)
    target = lax.broadcasted_iota(jnp.int32, (window.shape[1], 2 * PAD), 1)
    lane = jnp.where(target >= PAD, target - PAD, target)
    start = jnp.where(target >= PAD, offset + HEAD, offset)
    chosen = ((source == start + lane) & (lane < HEAD)).astype(F32).astype(BF16)
    return jnp.dot(window, chosen, preferred_element_type=F32).astype(BF16)


def project_kernel(place, *refs):
    packs, others, (w_qkv, w_out) = refs[:8], refs[8:16], refs[16:18]
    normed_out, q_out, k_out, v_out, g_out, wo = refs[18:]
    at_x, at_zh, at_c = place[0], place[1], place[4]
    nx = normed_out.shape[1]
    heads = q_out.shape[0]
    width = w_out.shape[0]
    first = (at_x * 2 + at_c) * heads * HEAD
    start = jnp.minimum(lax.div(first, PAD) * PAD, width - 2 * PAD)
    weights = []
    for kind in range(3):
        lanes = pl.ds(pl.multiple_of(kind * width + start, PAD), 2 * PAD)
        weights.append(select_heads(w_qkv[:, lanes], first - start))
    wkv = jnp.concatenate(weights[1:], axis=1)
    wo[...] = jnp.zeros_like(wo)
    for h in range(heads):
        wo[h * PAD : h * PAD + HEAD] = w_out[pl.ds(pl.multiple_of(first + h * HEAD, 16), HEAD), :]
    for twin in range(2):
        sample = lax.rem(at_c + twin, 2)
        for shift in range(nx):
            pack, other = packs[twin * nx + shift], others[twin * nx + shift]
            slot = lax.rem(at_x + shift, nx)
            mine = normalise(pack[0].astype(F32))
            far = normalise(other[0].astype(F32))
            normed_out[sample, slot, at_zh] = mine
            normed_out[sample, slot, 1 - at_zh] = far
            queries = jnp.dot(mine, weights[0], preferred_element_type=F32).astype(BF16)
            grad_att = right_transposed(pack[1], wo[...]).astype(BF16)
            for zh, tokens in ((at_zh, mine), (1 - at_zh, far)):
                keys_values = jnp.dot(tokens, wkv, preferred_element_type=F32).astype(BF16)
                for h in range(heads):
                    k_out[h, sample, slot, zh] = keys_values[:, h * PAD : (h + 1) * PAD]
                    v_out[h, sample, slot, zh] = keys_values[:, (heads + h) * PAD : (heads + h + 1) * PAD]
            for h in range(heads):
                q_out[h, sample, slot] = queries[:, h * PAD : (h + 1) * PAD]
                g_out[h, sample, slot] = grad_att[:, h * PAD : (h + 1) * PAD]


def project(place, packs, others, w_qkv, w_out, heads):
    _, rows, width = packs[0].shape
    nx = len(packs) // 2
    query_shape = jax.ShapeDtypeStruct((heads, 2, nx, rows, PAD), BF16)
    key_shape = jax.ShapeDtypeStruct((heads, 2, nx, 2, rows, PAD), BF16)
    whole = pl.BlockSpec(memory_space=pltpu.VMEM)
    return pl.pallas_call(
        project_kernel,
        in_specs=[pl.BlockSpec(memory_space=pltpu.SMEM)] + [whole] * 18,
        out_specs=[whole] * 5,
        out_shape=[
            jax.ShapeDtypeStruct((2, nx, 2, rows, width), BF16),
            query_shape,
            key_shape,
            key_shape,
            query_shape,
        ],
        scratch_shapes=[pltpu.VMEM((heads * PAD, width), BF16)],
        compiler_params=pltpu.CompilerParams(vmem_limit_bytes=VMEM_LIMIT),
        cost_estimate=cost(10),
        name="project",
    )(place, *packs, *others, w_qkv, w_out)


def weights_kernel(place, sent, normed, *refs):
    packs, outs, (turned, out_acc, piece) = refs[:8], refs[8:12], refs[12:]
    at_x, at_zh, at_y, at_c = place[0], place[1], place[2], place[4]
    nx, _, heads, _, rows = sent.shape
    width = normed.shape[-1]
    ny = len(outs)
    sums = [None] * 3
    for twin in range(2):
        s = lax.rem(at_c + twin, 2)

        def rows_of(x, slot):
            return [sent[x, s, h, slot * HEAD : (slot + 1) * HEAD, :] for h in range(heads)]

        def stacked(x, slots):
            return jnp.concatenate([r for slot in slots for r in rows_of(x, slot)], axis=0)

        kv_left = jnp.concatenate(
            [stacked(x, (2 + 2 * zh, 3 + 2 * zh)) for x in range(nx) for zh in range(2)], axis=1
        )
        q_left = jnp.concatenate([stacked(x, (1,)) for x in range(nx)], axis=1)
        slots = [lax.rem(at_x + shift, nx) for shift in range(nx)]
        out_left = jnp.concatenate([stacked(x, (0,)) for x in slots], axis=1)
        q_right = jnp.concatenate([normed[s, x, at_zh] for x in range(nx)], axis=0)
        out_right = jnp.concatenate([packs[twin * nx + shift][0] for shift in range(nx)], axis=0)
        terms = (
            jnp.dot(q_left, q_right, preferred_element_type=F32),
            jnp.dot(kv_left, normed[s].reshape(nx * 2 * rows, width), preferred_element_type=F32),
            jnp.dot(out_left, out_right, preferred_element_type=F32),
        )
        sums = [t if a is None else a + t for a, t in zip(sums, terms)]
    part = heads * HEAD
    blank = jnp.zeros((PAD - part, width), F32)
    for kind, block in enumerate((sums[0], sums[1][:part], sums[1][part:])):
        turned[:, kind * PAD : (kind + 1) * PAD] = jnp.concatenate([block, blank], axis=0).T
    out_acc[...] = sums[2]
    three = part // ny
    halfway = width // 2
    for shift in range(ny):
        low = lax.rem(at_y + shift, ny) * three
        count = width // part
        for j in range(count):
            piece[j * three : (j + 1) * three] = turned[pl.ds(pl.multiple_of(j * part + low, 8), three), :]
        for j in range(2):
            piece[(count + j) * three : (count + j + 1) * three] = out_acc[
                pl.ds(pl.multiple_of(low, 8), three), j * halfway : (j + 1) * halfway
            ]
        outs[shift][...] = piece[...].astype(BF16)


def weight_grads(place, sent, normed, packs, ny):
    width = normed.shape[-1]
    heads, rows = sent.shape[2], sent.shape[4]
    part = heads * HEAD
    height = (width // part + 2) * (part // ny)
    whole = pl.BlockSpec(memory_space=pltpu.VMEM)
    cot_spec = pl.BlockSpec((1, rows, width), lambda i: (1, 0, 0))
    full = lambda a: pl.BlockSpec(a.shape, lambda i: (0,) * a.ndim)
    out = jax.ShapeDtypeStruct((height, 3 * PAD), BF16)
    return pl.pallas_call(
        weights_kernel,
        grid=(1,),
        in_specs=[pl.BlockSpec(memory_space=pltpu.SMEM), full(sent), full(normed)] + [cot_spec] * len(packs),
        out_specs=[pl.BlockSpec((height, 3 * PAD), lambda i: (0, 0))] * ny,
        out_shape=[out] * ny,
        scratch_shapes=[
            pltpu.VMEM((width, 3 * PAD), F32),
            pltpu.VMEM((part, width), F32),
            pltpu.VMEM((height, 3 * PAD), F32),
        ],
        compiler_params=pltpu.CompilerParams(vmem_limit_bytes=VMEM_LIMIT),
        cost_estimate=cost(6),
        name="weight_grads",
    )(place, sent, normed, *packs)


def attention_kernel(scale, place, q_ref, k_ref, v_ref, g_ref, *refs):
    bias_refs, refs = refs[:4], refs[4:]
    send_ref, pair_refs, (bias, pair, dk_acc, dv_acc) = refs[0], refs[1:5], refs[5:]
    step = pl.program_id(0)
    at_y = place[2]
    wide = q_ref.shape[2]
    rows = q_ref.shape[3]
    ny = len(bias_refs)
    chunk = rows // ny
    total = k_ref.shape[2]
    spots = []
    for x in range(wide):
        for shift in range(ny):
            start = x * rows + lax.rem(at_y + shift, ny) * chunk
            spots.append((x, shift, pl.ds(pl.multiple_of(start, chunk), chunk)))

    @pl.when(step == 0)
    def _():
        dk_acc[...] = jnp.zeros_like(dk_acc)
        dv_acc[...] = jnp.zeros_like(dv_acc)

    for x, shift, spot in spots:
        bias[spot, :] = bias_refs[shift][x]
    for s in range(2):
        q = q_ref[0, s].reshape(wide * rows, PAD)
        g = g_ref[0, s].reshape(wide * rows, PAD)
        k, v = k_ref[0, s], v_ref[0, s]
        scores = right_transposed(q, k) * scale + bias[...].astype(F32)
        peak = jnp.max(scores, axis=-1, keepdims=True)
        expo = jnp.exp(scores - peak)
        probs = expo * (1.0 / jnp.sum(expo, axis=-1, keepdims=True))
        probs_b = probs.astype(BF16)
        att = jnp.dot(probs_b, v, preferred_element_type=F32).T
        grad_prob = right_transposed(g, v)
        centre = jnp.sum(probs * grad_prob, axis=-1, keepdims=True)
        grad_score = probs * (grad_prob - centre)
        score_b = grad_score.astype(BF16)
        if s == 0:
            pair[...] = grad_score
        else:
            pair[...] += grad_score
        dq = (jnp.dot(score_b, k, preferred_element_type=F32) * scale).T
        dk_acc[s] += jnp.dot(q.T, score_b, preferred_element_type=F32)
        dv_acc[s] += jnp.dot(g.T, probs_b, preferred_element_type=F32)
        for x in range(wide):
            send_ref[step * wide + x, s, 0, :HEAD] = att[:HEAD, x * rows : (x + 1) * rows].astype(BF16)
            send_ref[step * wide + x, s, 0, HEAD : 2 * HEAD] = dq[:HEAD, x * rows : (x + 1) * rows].astype(BF16)
    for x, shift, spot in spots:
        pair_refs[shift][x] = pair[spot, :].astype(BF16)

    @pl.when(step == pl.num_programs(0) - 1)
    def _():
        for s in range(2):
            for at in range(total // rows):
                x, zh = at // 2, at % 2
                low = (2 + 2 * zh) * HEAD
                lanes = slice(at * rows, (at + 1) * rows)
                send_ref[x, s, 0, low : low + HEAD] = (dk_acc[s, :HEAD, lanes] * scale).astype(BF16)
                send_ref[x, s, 0, low + HEAD : low + 2 * HEAD] = dv_acc[s, :HEAD, lanes].astype(BF16)


def attention(head, place, queries, keys, values, grad_att, bias, sent, scale):
    heads, _, nx, rows, _ = queries.shape
    total = keys.shape[2]
    wide = 2
    chunk = bias[0].shape[1]
    smem = pl.BlockSpec(memory_space=pltpu.SMEM)
    q_spec = pl.BlockSpec((1, 2, wide, rows, PAD), lambda i: (head, 0, i, 0, 0))
    k_spec = pl.BlockSpec((1, 2, total, PAD), lambda i: (head, 0, 0, 0))
    bias_spec = pl.BlockSpec((wide, chunk, total), lambda i: (i, 0, 0))
    send_shape = jax.ShapeDtypeStruct((nx, 2, heads, 6 * HEAD, rows), BF16)
    send_spec = pl.BlockSpec((nx, 2, 1, 6 * HEAD, rows), lambda i: (0, 0, head, 0, 0))
    pair_shape = jax.ShapeDtypeStruct(bias[0].shape, BF16)
    args = [place, queries, keys, values, grad_att, *bias]
    in_specs = [smem, q_spec, k_spec, k_spec, q_spec] + [bias_spec] * 4
    aliases = {}
    if sent is not None:
        aliases = {len(args): 0}
        args.append(sent)
        in_specs.append(pl.BlockSpec(memory_space=pl.ANY))

    def body(*refs):
        if sent is not None:
            refs = refs[:9] + refs[10:]
        attention_kernel(scale, *refs)

    return pl.pallas_call(
        body,
        grid=(nx // wide,),
        in_specs=in_specs,
        out_specs=[send_spec] + [bias_spec] * 4,
        out_shape=[send_shape] + [pair_shape] * 4,
        scratch_shapes=[
            pltpu.VMEM((wide * rows, total), BF16),
            pltpu.VMEM((wide * rows, total), F32),
            pltpu.VMEM((2, PAD, total), F32),
            pltpu.VMEM((2, PAD, total), F32),
        ],
        input_output_aliases=aliases,
        compiler_params=pltpu.CompilerParams(vmem_limit_bytes=VMEM_LIMIT),
        cost_estimate=cost(9),
        name="attention",
    )(*args)


def exchange(values, axes):
    return lax.all_to_all(values, axes, split_axis=0, concat_axis=0, tiled=True)


def ring(n, shift):
    return [(i, (i + shift) % n) for i in range(n)]


def ring_gather(values, up, down, via_up):
    low, high = lax.ppermute(values, "y", up), lax.ppermute(values, "y", down)
    far = lax.ppermute(low, "y", up) if via_up else lax.ppermute(high, "y", down)
    return values, high, far, low


def ring_scatter(pieces, up, down, via_up):
    base, high, far, low = pieces
    if via_up:
        high = (high.astype(F32) + lax.ppermute(far, "y", up).astype(F32)).astype(BF16)
    else:
        low = (low.astype(F32) + lax.ppermute(far, "y", down).astype(F32)).astype(BF16)
    got = lax.ppermute(high, "y", up).astype(F32) + lax.ppermute(low, "y", down).astype(F32)
    return base.astype(F32) + got


def per_device(activations, pair_bias, w_qkv, w_out, cotangent):
    act = activations[0]
    cot = cotangent[0]
    rows, width = act.shape
    nx, nzh, ny, nzl, nc = (lax.axis_size(a) for a in AXES)
    place = jnp.stack([lax.axis_index(a) for a in AXES]).astype(jnp.int32)
    at_x, at_zh, at_c = place[0], place[1], place[4]
    groups = nx * nc
    heads = H // groups
    part = width // groups
    scale = 1.0 / math.sqrt(HEAD)
    total = pair_bias.shape[2]
    own_rows = pair_bias.shape[1]
    chunk = nzl * nc * own_rows
    swap = [(0, 1), (1, 0)]
    up, down = ring(ny, 1), ring(ny, -1)

    def around_x(values):
        from_low = lax.ppermute(values, "x", ring(nx, 1))
        from_high = lax.ppermute(values, "x", ring(nx, -1))
        relay = jnp.where(at_c == 0, from_low, from_high)
        pairs = []
        for i in range(nx):
            pairs.append((i * nc, ((i + 1) % nx) * nc))
            pairs.append((i * nc + 1, ((i - 1) % nx) * nc + 1))
        from_far = lax.ppermute(relay, ("x", "c"), pairs)
        pieces = [values, from_high, from_far, from_low]
        return pieces + [lax.ppermute(piece, "c", swap) for piece in pieces]

    with jax.named_scope("gather"):
        act_other = lax.ppermute(act, "zh", swap)
        packs = around_x(jnp.stack([act, cot]))
        others = around_x(act_other[None])

    with jax.named_scope("bias_in"):
        bias = []
        for h in range(heads):
            send = pair_bias.reshape(nx, 1, nc, heads, own_rows, total)[:, :, :, h]
            send = jnp.broadcast_to(send, (nx, nzl, nc, own_rows, total))
            got = exchange(send.reshape(nx * nzl * nc, own_rows, total), ("x", "zl", "c"))
            bias.append(ring_gather(got.reshape(nx, chunk, total), up, down, h % 2 == 0))

    with jax.named_scope("project"):
        normed_all, queries, keys, values, grad_att = project(place, packs, others, w_qkv, w_out, heads)
        keys = keys.reshape(heads, 2, total, PAD)
        values = values.reshape(heads, 2, total, PAD)

    sent = None
    pairs_out = []
    with jax.named_scope("attention"):
        for h in range(heads):
            sent, *pair = attention(h, place, queries, keys, values, grad_att, bias[h], sent, scale)
            pairs_out.append(pair)

    with jax.named_scope("weights"):
        weight_pieces = weight_grads(place, sent, normed_all, packs, ny)

    with jax.named_scope("along_y"):
        sums = [ring_scatter(pair, up, down, h % 2 == 0) for h, pair in enumerate(pairs_out)]
        sums = [v.astype(BF16).reshape(nx * nzl * nc, own_rows, total) for v in sums]
        weight_sum = ring_scatter(weight_pieces, up, down, False).astype(BF16)

    with jax.named_scope("owners"):
        three = width // (nx * nzh * ny * nzl * nc)
        cut = nx * nzh * nzl * nc * three
        qkv_part = weight_sum[:cut].reshape(nx, nzh, nzl, nc, three, 3 * PAD).transpose(0, 2, 3, 1, 4, 5)
        out_part = weight_sum[cut:].reshape(1, 2, nzl, nc, three, width // 2).transpose(0, 2, 3, 1, 4, 5)
        here = (jnp.arange(nx) == at_x).reshape(nx, 1, 1, 1, 1, 1)
        out_part = jnp.where(here, out_part, jnp.zeros_like(out_part))
        peers = nx * nzl * nc
        weight_send = jnp.concatenate(
            [qkv_part.reshape(peers, -1), out_part.reshape(peers, -1)], axis=1
        ).reshape(peers, heads * own_rows, -1)
        pair_send = jnp.concatenate(sums, axis=1)
        got = exchange(jnp.concatenate([pair_send, weight_send], axis=2), ("x", "zl", "c"))
        pair_got = got[:, :, :total].reshape(nx, nzl, nc, heads, own_rows, total).astype(F32)
        grad_pair = jnp.sum(pair_got, axis=1).astype(BF16).reshape(H, own_rows, total)
        weight_got = jnp.sum(got[:, :, total:].reshape(nx, nzl, nc, -1).astype(F32), axis=1)
        cut = nzh * three * 3 * PAD
        qkv_part = weight_got[:, :, :cut].reshape(groups, nzh, three, 3, PAD)[..., :part]
        qkv_part = qkv_part.transpose(1, 2, 3, 0, 4).reshape(nzh, three, 3 * width)
        out_part = jnp.sum(weight_got[:, :, cut:], axis=0).reshape(nzh, 2, three, width // 2)
        out_part = out_part.transpose(0, 2, 1, 3).reshape(nzh, three, width)
        partial = jnp.concatenate([qkv_part, out_part], axis=2)
        away = lax.dynamic_index_in_dim(partial, 1 - at_zh, 0, keepdims=False).astype(BF16)
        grad_weights = lax.dynamic_index_in_dim(partial, at_zh, 0, keepdims=False)
        grad_weights = grad_weights + lax.ppermute(away, "zh", swap).astype(F32)

    with jax.named_scope("tokens_out"):
        got = exchange(sent.reshape(groups, heads * 6 * HEAD, rows), ("x", "c"))
        got = got.reshape(groups, heads, 6, HEAD, rows)
        attended = got[:, :, 0].reshape(width, rows)
        grad_query = got[:, :, 1].reshape(width, rows)
        grad_kv = got[:, :, 2:].reshape(groups, heads, nzh, 2, HEAD, rows).transpose(2, 3, 0, 1, 4, 5)
        grad_kv = grad_kv.reshape(nzh, 2 * width, rows)
        kv_own = lax.dynamic_index_in_dim(grad_kv, at_zh, 0, keepdims=False)
        kv_other = lax.dynamic_index_in_dim(grad_kv, 1 - at_zh, 0, keepdims=False)

        def product(left, right, dims):
            return lax.dot_general(left, right, (dims, ((), ())), preferred_element_type=F32)

        grad_other = product(kv_other, w_qkv[:, width:], ((0,), (1,))).astype(BF16)
        grad_other = lax.ppermute(grad_other, "zh", swap)
        update = product(attended, w_out, ((0,), (0,))).astype(BF16)
        grad_own = product(jnp.concatenate([grad_query, kv_own], axis=0), w_qkv, ((0,), (1,)))
        normed, inverse = layer_norm(act.astype(F32))
        grad_act = norm_backward(grad_own + grad_other.astype(F32), normed, inverse).astype(BF16)

    return (update[None], grad_act[None], grad_pair, grad_weights)


def solution(mesh):
    fine = Mesh(mesh.devices.reshape(4, 2, 4, 4, 2), AXES)
    row, samp = ("x", "zh"), ("y", "zl", "c")
    in_specs = (
        P(samp, row, None),
        P(None, row + samp, None),
        P(),
        P(),
        P(samp, row, None),
    )
    out_specs = (
        P(samp, row, None),
        P(samp, row, None),
        P(None, row + samp, None),
        P(row + samp, None),
    )
    return jax.shard_map(
        per_device, mesh=fine, in_specs=in_specs, out_specs=out_specs, check_vma=False
    )
```

```python
import math

import jax
import jax.numpy as jnp
from jax import lax
from jax.experimental import pallas as pl
from jax.experimental.pallas import tpu as pltpu
from jax.sharding import Mesh, PartitionSpec as P

H = 16
HEAD = 48
PAD = 128
AXES = ("x", "zh", "y", "zl", "c")
VMEM_LIMIT = 56 * 1024 * 1024

epsilon = 1e-05
F32 = jnp.float32
BF16 = jnp.bfloat16


def layer_norm(values):
    mean_value = jnp.mean(values, axis=-1, keepdims=True)
    centred = values - mean_value
    variance = jnp.mean(centred * centred, axis=-1, keepdims=True)
    inverse = lax.rsqrt(variance + epsilon)
    return (centred * inverse, inverse)


def norm_backward(grad_in, normed, inverse):
    first_mean = jnp.mean(grad_in, axis=-1, keepdims=True)
    second_mean = jnp.mean(grad_in * normed, axis=-1, keepdims=True)
    return inverse * (grad_in - first_mean - normed * second_mean)


def right_transposed(left, right):
    return lax.dot_general(left, right, (((1,), (1,)), ((), ())), preferred_element_type=F32)


def normalise(values):
    mean_value = jnp.mean(values, axis=-1, keepdims=True)
    centred = values - mean_value
    variance = jnp.mean(centred * centred, axis=-1, keepdims=True)
    return (centred * lax.rsqrt(variance + epsilon)).astype(BF16)


def cost(us):
    return pl.CostEstimate(flops=int(us * 1e9), bytes_accessed=int(us * 3e6), transcendentals=0)


def select_heads(window, offset):
    source = lax.broadcasted_iota(jnp.int32, (window.shape[1], 2 * PAD), 0)
    target = lax.broadcasted_iota(jnp.int32, (window.shape[1], 2 * PAD), 1)
    lane = jnp.where(target >= PAD, target - PAD, target)
    start = jnp.where(target >= PAD, offset + HEAD, offset)
    chosen = ((source == start + lane) & (lane < HEAD)).astype(F32).astype(BF16)
    return jnp.dot(window, chosen, preferred_element_type=F32).astype(BF16)


def project_kernel(place, *refs):
    packs, (w_qkv, w_out) = refs[:8], refs[8:10]
    normed_out, q_out, k_out, v_out, g_out, wo = refs[10:]
    at_x, at_zh, at_c = place[0], place[1], place[4]
    nx = normed_out.shape[1]
    heads = q_out.shape[0]
    width = w_out.shape[0]
    first = (at_x * 2 + at_c) * heads * HEAD
    start = jnp.minimum(lax.div(first, PAD) * PAD, width - 2 * PAD)
    weights = []
    for kind in range(3):
        lanes = pl.ds(pl.multiple_of(kind * width + start, PAD), 2 * PAD)
        weights.append(select_heads(w_qkv[:, lanes], first - start))
    wkv = jnp.concatenate(weights[1:], axis=1)
    wo[...] = jnp.zeros_like(wo)
    for h in range(heads):
        wo[h * PAD : h * PAD + HEAD] = w_out[pl.ds(pl.multiple_of(first + h * HEAD, 16), HEAD), :]
    for twin in range(2):
        sample = lax.rem(at_c + twin, 2)
        for shift in range(nx):
            pack = packs[twin * nx + shift]
            slot = lax.rem(at_x + shift, nx)
            mine = normalise(pack[0].astype(F32))
            far = normalise(pack[1].astype(F32))
            normed_out[sample, slot, at_zh] = mine
            normed_out[sample, slot, 1 - at_zh] = far
            queries = jnp.dot(mine, weights[0], preferred_element_type=F32).astype(BF16)
            grad_att = right_transposed(pack[2], wo[...]).astype(BF16)
            for zh, tokens in ((at_zh, mine), (1 - at_zh, far)):
                keys_values = jnp.dot(tokens, wkv, preferred_element_type=F32).astype(BF16)
                for h in range(heads):
                    k_out[h, sample, slot, zh] = keys_values[:, h * PAD : (h + 1) * PAD]
                    v_out[h, sample, slot, zh] = keys_values[:, (heads + h) * PAD : (heads + h + 1) * PAD]
            for h in range(heads):
                q_out[h, sample, slot] = queries[:, h * PAD : (h + 1) * PAD]
                g_out[h, sample, slot] = grad_att[:, h * PAD : (h + 1) * PAD]


def project(place, packs, w_qkv, w_out, heads):
    _, rows, width = packs[0].shape
    nx = len(packs) // 2
    query_shape = jax.ShapeDtypeStruct((heads, 2, nx, rows, PAD), BF16)
    key_shape = jax.ShapeDtypeStruct((heads, 2, nx, 2, rows, PAD), BF16)
    whole = pl.BlockSpec(memory_space=pltpu.VMEM)
    return pl.pallas_call(
        project_kernel,
        in_specs=[pl.BlockSpec(memory_space=pltpu.SMEM)] + [whole] * 10,
        out_specs=[whole] * 5,
        out_shape=[
            jax.ShapeDtypeStruct((2, nx, 2, rows, width), BF16),
            query_shape,
            key_shape,
            key_shape,
            query_shape,
        ],
        scratch_shapes=[pltpu.VMEM((heads * PAD, width), BF16)],
        compiler_params=pltpu.CompilerParams(vmem_limit_bytes=VMEM_LIMIT),
        cost_estimate=cost(10),
        name="project",
    )(place, *packs, w_qkv, w_out)


def weights_kernel(place, sent, normed, *refs):
    packs, outs, (turned, out_acc, piece) = refs[:8], refs[9:13], refs[13:]
    at_x, at_zh, at_y, at_c = place[0], place[1], place[2], place[4]
    nx, _, heads, _, rows = sent.shape
    width = normed.shape[-1]
    ny = len(outs)
    sums = [None] * 3
    for twin in range(2):
        s = lax.rem(at_c + twin, 2)

        def rows_of(x, slot):
            return [sent[x, s, h, slot * HEAD : (slot + 1) * HEAD, :] for h in range(heads)]

        def stacked(x, slots):
            return jnp.concatenate([r for slot in slots for r in rows_of(x, slot)], axis=0)

        kv_left = jnp.concatenate(
            [stacked(x, (2 + 2 * zh, 3 + 2 * zh)) for x in range(nx) for zh in range(2)], axis=1
        )
        q_left = jnp.concatenate([stacked(x, (1,)) for x in range(nx)], axis=1)
        slots = [lax.rem(at_x + shift, nx) for shift in range(nx)]
        out_left = jnp.concatenate([stacked(x, (0,)) for x in slots], axis=1)
        q_right = jnp.concatenate([normed[s, x, at_zh] for x in range(nx)], axis=0)
        out_right = jnp.concatenate([packs[twin * nx + shift][0] for shift in range(nx)], axis=0)
        terms = (
            jnp.dot(q_left, q_right, preferred_element_type=F32),
            jnp.dot(kv_left, normed[s].reshape(nx * 2 * rows, width), preferred_element_type=F32),
            jnp.dot(out_left, out_right, preferred_element_type=F32),
        )
        sums = [t if a is None else a + t for a, t in zip(sums, terms)]
    part = heads * HEAD
    blank = jnp.zeros((PAD - part, width), F32)
    for kind, block in enumerate((sums[0], sums[1][:part], sums[1][part:])):
        turned[:, kind * PAD : (kind + 1) * PAD] = jnp.concatenate([block, blank], axis=0).T
    out_acc[...] = sums[2]
    three = part // ny
    halfway = width // 2
    for shift in range(ny):
        low = lax.rem(at_y + shift, ny) * three
        count = width // part
        for j in range(count):
            piece[j * three : (j + 1) * three] = turned[pl.ds(pl.multiple_of(j * part + low, 8), three), :]
        for j in range(2):
            piece[(count + j) * three : (count + j + 1) * three] = out_acc[
                pl.ds(pl.multiple_of(low, 8), three), j * halfway : (j + 1) * halfway
            ]
        outs[shift][...] = piece[...].astype(BF16)


def weight_grads(place, sent, normed, packs, ny, after):
    width = normed.shape[-1]
    heads, rows = sent.shape[2], sent.shape[4]
    part = heads * HEAD
    height = (width // part + 2) * (part // ny)
    whole = pl.BlockSpec(memory_space=pltpu.VMEM)
    cot_spec = pl.BlockSpec((1, rows, width), lambda i: (2, 0, 0))
    full = lambda a: pl.BlockSpec(a.shape, lambda i: (0,) * a.ndim)
    out = jax.ShapeDtypeStruct((height, 3 * PAD), BF16)
    return pl.pallas_call(
        weights_kernel,
        grid=(1,),
        in_specs=[pl.BlockSpec(memory_space=pltpu.SMEM), full(sent), full(normed)] + [cot_spec] * len(packs) + [pl.BlockSpec(memory_space=pl.ANY)],
        out_specs=[pl.BlockSpec((height, 3 * PAD), lambda i: (0, 0))] * ny,
        out_shape=[out] * ny,
        scratch_shapes=[
            pltpu.VMEM((width, 3 * PAD), F32),
            pltpu.VMEM((part, width), F32),
            pltpu.VMEM((height, 3 * PAD), F32),
        ],
        compiler_params=pltpu.CompilerParams(vmem_limit_bytes=VMEM_LIMIT),
        cost_estimate=cost(6),
        name="weight_grads",
    )(place, sent, normed, *packs, after)


def attention_kernel(scale, place, q_ref, k_ref, v_ref, g_ref, *refs):
    bias_refs, refs = refs[:4], refs[4:]
    send_ref, pair_refs, (bias, pair, dk_acc, dv_acc) = refs[0], refs[1:5], refs[5:]
    step = pl.program_id(0)
    at_y = place[2]
    wide = q_ref.shape[2]
    rows = q_ref.shape[3]
    ny = len(bias_refs)
    chunk = rows // ny
    total = k_ref.shape[2]
    spots = []
    for x in range(wide):
        for shift in range(ny):
            start = x * rows + lax.rem(at_y + shift, ny) * chunk
            spots.append((x, shift, pl.ds(pl.multiple_of(start, chunk), chunk)))

    @pl.when(step == 0)
    def _():
        dk_acc[...] = jnp.zeros_like(dk_acc)
        dv_acc[...] = jnp.zeros_like(dv_acc)

    for x, shift, spot in spots:
        bias[spot, :] = bias_refs[shift][x]
    for s in range(2):
        q = q_ref[0, s].reshape(wide * rows, PAD)
        g = g_ref[0, s].reshape(wide * rows, PAD)
        k, v = k_ref[0, s], v_ref[0, s]
        scores = right_transposed(q, k) * scale + bias[...].astype(F32)
        peak = jnp.max(scores, axis=-1, keepdims=True)
        expo = jnp.exp(scores - peak)
        probs = expo * (1.0 / jnp.sum(expo, axis=-1, keepdims=True))
        probs_b = probs.astype(BF16)
        att = jnp.dot(probs_b, v, preferred_element_type=F32).T
        grad_prob = right_transposed(g, v)
        centre = jnp.sum(probs * grad_prob, axis=-1, keepdims=True)
        grad_score = probs * (grad_prob - centre)
        score_b = grad_score.astype(BF16)
        if s == 0:
            pair[...] = grad_score
        else:
            pair[...] += grad_score
        dq = (jnp.dot(score_b, k, preferred_element_type=F32) * scale).T
        dk_acc[s] += jnp.dot(q.T, score_b, preferred_element_type=F32)
        dv_acc[s] += jnp.dot(g.T, probs_b, preferred_element_type=F32)
        for x in range(wide):
            send_ref[step * wide + x, s, 0, :HEAD] = att[:HEAD, x * rows : (x + 1) * rows].astype(BF16)
            send_ref[step * wide + x, s, 0, HEAD : 2 * HEAD] = dq[:HEAD, x * rows : (x + 1) * rows].astype(BF16)
    for x, shift, spot in spots:
        pair_refs[shift][x] = pair[spot, :].astype(BF16)

    @pl.when(step == pl.num_programs(0) - 1)
    def _():
        for s in range(2):
            for at in range(total // rows):
                x, zh = at // 2, at % 2
                low = (2 + 2 * zh) * HEAD
                lanes = slice(at * rows, (at + 1) * rows)
                send_ref[x, s, 0, low : low + HEAD] = (dk_acc[s, :HEAD, lanes] * scale).astype(BF16)
                send_ref[x, s, 0, low + HEAD : low + 2 * HEAD] = dv_acc[s, :HEAD, lanes].astype(BF16)


def attention(head, place, queries, keys, values, grad_att, bias, sent, scale):
    heads, _, nx, rows, _ = queries.shape
    total = keys.shape[2]
    wide = 2
    chunk = bias[0].shape[1]
    smem = pl.BlockSpec(memory_space=pltpu.SMEM)
    q_spec = pl.BlockSpec((1, 2, wide, rows, PAD), lambda i: (head, 0, i, 0, 0))
    k_spec = pl.BlockSpec((1, 2, total, PAD), lambda i: (head, 0, 0, 0))
    bias_spec = pl.BlockSpec((wide, chunk, total), lambda i: (i, 0, 0))
    send_shape = jax.ShapeDtypeStruct((nx, 2, heads, 6 * HEAD, rows), BF16)
    send_spec = pl.BlockSpec((nx, 2, 1, 6 * HEAD, rows), lambda i: (0, 0, head, 0, 0))
    pair_shape = jax.ShapeDtypeStruct(bias[0].shape, BF16)
    args = [place, queries, keys, values, grad_att, *bias]
    in_specs = [smem, q_spec, k_spec, k_spec, q_spec] + [bias_spec] * 4
    aliases = {}
    if sent is not None:
        aliases = {len(args): 0}
        args.append(sent)
        in_specs.append(pl.BlockSpec(memory_space=pl.ANY))

    def body(*refs):
        if sent is not None:
            refs = refs[:9] + refs[10:]
        attention_kernel(scale, *refs)

    return pl.pallas_call(
        body,
        grid=(nx // wide,),
        in_specs=in_specs,
        out_specs=[send_spec] + [bias_spec] * 4,
        out_shape=[send_shape] + [pair_shape] * 4,
        scratch_shapes=[
            pltpu.VMEM((wide * rows, total), BF16),
            pltpu.VMEM((wide * rows, total), F32),
            pltpu.VMEM((2, PAD, total), F32),
            pltpu.VMEM((2, PAD, total), F32),
        ],
        input_output_aliases=aliases,
        compiler_params=pltpu.CompilerParams(vmem_limit_bytes=VMEM_LIMIT),
        cost_estimate=cost(9),
        name="attention",
    )(*args)


def exchange(values, axes):
    return lax.all_to_all(values, axes, split_axis=0, concat_axis=0, tiled=True)


def ring(n, shift):
    return [(i, (i + shift) % n) for i in range(n)]


def around(values, axis):
    n = lax.axis_size(axis)
    return [values] + [lax.ppermute(values, axis, ring(n, -shift)) for shift in range(1, n)]


def ring_scatter(pieces, axis):
    n = lax.axis_size(axis)
    total = pieces[0].astype(F32)
    for shift in range(1, n):
        total = total + lax.ppermute(pieces[shift], axis, ring(n, shift)).astype(F32)
    return total


def per_device(activations, pair_bias, w_qkv, w_out, cotangent):
    act = activations[0]
    cot = cotangent[0]
    rows, width = act.shape
    nx, nzh, ny, nzl, nc = (lax.axis_size(a) for a in AXES)
    place = jnp.stack([lax.axis_index(a) for a in AXES]).astype(jnp.int32)
    at_x, at_zh, at_c = place[0], place[1], place[4]
    groups = nx * nc
    heads = H // groups
    part = width // groups
    scale = 1.0 / math.sqrt(HEAD)
    total = pair_bias.shape[2]
    own_rows = pair_bias.shape[1]
    chunk = nzl * nc * own_rows
    swap = [(0, 1), (1, 0)]

    def gather(values):
        pieces = around(values, "x")
        return pieces + [lax.ppermute(piece, "c", swap) for piece in pieces]

    with jax.named_scope("gather"):
        act_other = lax.ppermute(act, "zh", swap)
        packs = gather(jnp.stack([act, act_other, cot]))

    with jax.named_scope("bias_in"):
        send = pair_bias.reshape(nx, 1, nc, heads, own_rows, total)
        send = jnp.broadcast_to(send, (nx, nzl, nc, heads, own_rows, total))
        got = exchange(send.reshape(nx * nzl * nc, heads, own_rows, total), ("x", "zl", "c"))
        got = got.reshape(nx, nzl * nc, heads, own_rows, total)
        bias = [around(got[:, :, h].reshape(nx, chunk, total), "y") for h in range(heads)]

    with jax.named_scope("project"):
        normed_all, queries, keys, values, grad_att = project(place, packs, w_qkv, w_out, heads)
        keys = keys.reshape(heads, 2, total, PAD)
        values = values.reshape(heads, 2, total, PAD)

    sent = None
    pairs_out = []
    with jax.named_scope("attention"):
        for h in range(heads):
            sent, *pair = attention(h, place, queries, keys, values, grad_att, bias[h], sent, scale)
            pairs_out.append(pair)

    with jax.named_scope("along_y"):
        sums = [ring_scatter(pair, "y").astype(BF16) for pair in pairs_out]

    with jax.named_scope("weights"):
        weight_pieces = weight_grads(place, sent, normed_all, packs, ny, sums[0])

    with jax.named_scope("along_y"):
        sums = [v.reshape(nx * nzl * nc, own_rows, total) for v in sums]
        weight_sum = ring_scatter(weight_pieces, "y").astype(BF16)

    with jax.named_scope("owners"):
        three = width // (nx * nzh * ny * nzl * nc)
        cut = nx * nzh * nzl * nc * three
        qkv_part = weight_sum[:cut].reshape(nx, nzh, nzl, nc, three, 3 * PAD).transpose(0, 2, 3, 1, 4, 5)
        out_part = weight_sum[cut:].reshape(1, 2, nzl, nc, three, width // 2).transpose(0, 2, 3, 1, 4, 5)
        here = (jnp.arange(nx) == at_x).reshape(nx, 1, 1, 1, 1, 1)
        out_part = jnp.where(here, out_part, jnp.zeros_like(out_part))
        peers = nx * nzl * nc
        weight_send = jnp.concatenate(
            [qkv_part.reshape(peers, -1), out_part.reshape(peers, -1)], axis=1
        ).reshape(peers, heads * own_rows, -1)
        pair_send = jnp.concatenate(sums, axis=1)
        got = exchange(jnp.concatenate([pair_send, weight_send], axis=2), ("x", "zl", "c"))
        pair_got = got[:, :, :total].reshape(nx, nzl, nc, heads, own_rows, total).astype(F32)
        grad_pair = jnp.sum(pair_got, axis=1).astype(BF16).reshape(H, own_rows, total)
        weight_got = jnp.sum(got[:, :, total:].reshape(nx, nzl, nc, -1).astype(F32), axis=1)
        cut = nzh * three * 3 * PAD
        qkv_part = weight_got[:, :, :cut].reshape(groups, nzh, three, 3, PAD)[..., :part]
        qkv_part = qkv_part.transpose(1, 2, 3, 0, 4).reshape(nzh, three, 3 * width)
        out_part = jnp.sum(weight_got[:, :, cut:], axis=0).reshape(nzh, 2, three, width // 2)
        out_part = out_part.transpose(0, 2, 1, 3).reshape(nzh, three, width)
        partial = jnp.concatenate([qkv_part, out_part], axis=2)
        away = lax.dynamic_index_in_dim(partial, 1 - at_zh, 0, keepdims=False).astype(BF16)
        grad_weights = lax.dynamic_index_in_dim(partial, at_zh, 0, keepdims=False)
        grad_weights = grad_weights + lax.ppermute(away, "zh", swap).astype(F32)

    with jax.named_scope("tokens_out"):
        got = exchange(sent.reshape(groups, heads * 6 * HEAD, rows), ("x", "c"))
        got = got.reshape(groups, heads, 6, HEAD, rows)
        attended = got[:, :, 0].reshape(width, rows)
        grad_query = got[:, :, 1].reshape(width, rows)
        grad_kv = got[:, :, 2:].reshape(groups, heads, nzh, 2, HEAD, rows).transpose(2, 3, 0, 1, 4, 5)
        grad_kv = grad_kv.reshape(nzh, 2 * width, rows)
        kv_own = lax.dynamic_index_in_dim(grad_kv, at_zh, 0, keepdims=False)
        kv_other = lax.dynamic_index_in_dim(grad_kv, 1 - at_zh, 0, keepdims=False)

        def product(left, right, dims):
            return lax.dot_general(left, right, (dims, ((), ())), preferred_element_type=F32)

        grad_other = product(kv_other, w_qkv[:, width:], ((0,), (1,))).astype(BF16)
        grad_other = lax.ppermute(grad_other, "zh", swap)
        update = product(attended, w_out, ((0,), (0,))).astype(BF16)
        grad_own = product(jnp.concatenate([grad_query, kv_own], axis=0), w_qkv, ((0,), (1,)))
        normed, inverse = layer_norm(act.astype(F32))
        grad_act = norm_backward(grad_own + grad_other.astype(F32), normed, inverse).astype(BF16)

    return (update[None], grad_act[None], grad_pair, grad_weights)


def solution(mesh):
    fine = Mesh(mesh.devices.reshape(4, 2, 4, 4, 2), AXES)
    row, samp = ("x", "zh"), ("y", "zl", "c")
    in_specs = (
        P(samp, row, None),
        P(None, row + samp, None),
        P(),
        P(),
        P(samp, row, None),
    )
    out_specs = (
        P(samp, row, None),
        P(samp, row, None),
        P(None, row + samp, None),
        P(row + samp, None),
    )
    return jax.shard_map(
        per_device, mesh=fine, in_specs=in_specs, out_specs=out_specs, check_vma=False
    )
```

```python
import math

import jax
import jax.numpy as jnp
from jax import lax
from jax.experimental import pallas as pl
from jax.experimental.pallas import tpu as pltpu
from jax.sharding import Mesh, PartitionSpec as P

H = 16
HEAD = 48
PAD = 128
AXES = ("x", "zh", "y", "zl", "c")
VMEM_LIMIT = 56 * 1024 * 1024

epsilon = 1e-05
F32 = jnp.float32
BF16 = jnp.bfloat16


def layer_norm(values):
    mean_value = jnp.mean(values, axis=-1, keepdims=True)
    centred = values - mean_value
    variance = jnp.mean(centred * centred, axis=-1, keepdims=True)
    inverse = lax.rsqrt(variance + epsilon)
    return (centred * inverse, inverse)


def norm_backward(grad_in, normed, inverse):
    first_mean = jnp.mean(grad_in, axis=-1, keepdims=True)
    second_mean = jnp.mean(grad_in * normed, axis=-1, keepdims=True)
    return inverse * (grad_in - first_mean - normed * second_mean)


def right_transposed(left, right):
    return lax.dot_general(left, right, (((1,), (1,)), ((), ())), preferred_element_type=F32)


def normalise(values):
    mean_value = jnp.mean(values, axis=-1, keepdims=True)
    centred = values - mean_value
    variance = jnp.mean(centred * centred, axis=-1, keepdims=True)
    return (centred * lax.rsqrt(variance + epsilon)).astype(BF16)


def cost(us):
    return pl.CostEstimate(flops=int(us * 1e9), bytes_accessed=int(us * 3e6), transcendentals=0)


def project_kernel(place, act, other, cot, w_qkv, w_out, *refs):
    outs, turned = refs[:-1], refs[-1]
    at_x = place[0]
    nx = len(outs)
    rows, width = act.shape
    mine = normalise(act[...].astype(F32))
    far = normalise(other[...].astype(F32))
    turned[: 3 * width] = jnp.dot(mine, w_qkv[...], preferred_element_type=F32).T.astype(BF16)
    turned[3 * width : 4 * width] = right_transposed(cot[...], w_out[...]).T.astype(BF16)
    turned[4 * width :] = jnp.dot(far, w_qkv[:, width:], preferred_element_type=F32).T.astype(BF16)
    kinds = turned.shape[0] // width
    cores, height, _ = outs[0].shape
    heads = height // (kinds * HEAD)
    for shift in range(nx):
        slot = lax.rem(at_x + shift, nx)
        for core in range(cores):
            for h in range(heads):
                for kind in range(kinds):
                    start = kind * width + ((slot * cores + core) * heads + h) * HEAD
                    row = (h * kinds + kind) * HEAD
                    outs[shift][core, row : row + HEAD] = turned[pl.ds(pl.multiple_of(start, 16), HEAD), :]


def project(place, act, other, cot, w_qkv, w_out, nx, nc):
    rows, width = act.shape
    kinds = 6
    whole = pl.BlockSpec(memory_space=pltpu.VMEM)
    out = jax.ShapeDtypeStruct((nc, kinds * width // (nx * nc), rows), BF16)
    return pl.pallas_call(
        project_kernel,
        in_specs=[pl.BlockSpec(memory_space=pltpu.SMEM)] + [whole] * 5,
        out_specs=[whole] * nx,
        out_shape=[out] * nx,
        scratch_shapes=[pltpu.VMEM((kinds * width, rows), BF16)],
        compiler_params=pltpu.CompilerParams(vmem_limit_bytes=VMEM_LIMIT),
        cost_estimate=cost(5),
        name="project",
    )(place, act, other, cot, w_qkv, w_out)


def pack_kernel(act, other, cot, *refs):
    out = refs[-1]
    out[0] = normalise(act[...].astype(F32))
    out[1] = normalise(other[...].astype(F32))
    out[2] = cot[...]


def pack(act, other, cot, after):
    whole = pl.BlockSpec(memory_space=pltpu.VMEM)
    return pl.pallas_call(
        pack_kernel,
        in_specs=[whole] * 3 + [pl.BlockSpec(memory_space=pl.ANY)] * len(after),
        out_specs=whole,
        out_shape=jax.ShapeDtypeStruct((3,) + act.shape, BF16),
        compiler_params=pltpu.CompilerParams(vmem_limit_bytes=VMEM_LIMIT),
        cost_estimate=cost(2),
        name="pack",
    )(act, other, cot, *after)


def weights_kernel(place, *refs):
    sent, packs, outs, (turned, out_acc, piece) = refs[:2], refs[2:10], refs[11:15], refs[15:]
    at_x, at_zh, at_y, at_c = place[0], place[1], place[2], place[4]
    heads = len(sent)
    nx = sent[0].shape[0]
    width = packs[0].shape[-1]
    ny = len(outs)
    sums = [None] * 3

    def stacked(x, s, slots):
        return jnp.concatenate(
            [
                sent[h][x, s, pl.ds(pl.multiple_of(slot * HEAD, 16), HEAD), :]
                for slot in slots
                for h in range(heads)
            ],
            axis=0,
        )

    for twin in range(2):
        s = lax.rem(at_c + twin, 2)
        slots = [lax.rem(at_x + shift, nx) for shift in range(nx)]
        pieces = packs[twin * nx : (twin + 1) * nx]
        own, other = 2 + 2 * at_zh, 4 - 2 * at_zh
        kv_left = jnp.concatenate(
            [stacked(x, s, (own, own + 1)) for x in slots] + [stacked(x, s, (other, other + 1)) for x in slots],
            axis=1,
        )
        q_left = jnp.concatenate([stacked(x, s, (1,)) for x in slots], axis=1)
        out_left = jnp.concatenate([stacked(x, s, (0,)) for x in slots], axis=1)
        own_right = jnp.concatenate([p[0] for p in pieces], axis=0)
        other_right = jnp.concatenate([p[1] for p in pieces], axis=0)
        out_right = jnp.concatenate([p[2] for p in pieces], axis=0)
        terms = (
            jnp.dot(q_left, own_right, preferred_element_type=F32),
            jnp.dot(kv_left, jnp.concatenate([own_right, other_right], axis=0), preferred_element_type=F32),
            jnp.dot(out_left, out_right, preferred_element_type=F32),
        )
        sums = [t if a is None else a + t for a, t in zip(sums, terms)]
    part = heads * HEAD
    blank = jnp.zeros((PAD - part, width), F32)
    for kind, block in enumerate((sums[0], sums[1][:part], sums[1][part:])):
        turned[:, kind * PAD : (kind + 1) * PAD] = jnp.concatenate([block, blank], axis=0).T
    out_acc[...] = sums[2]
    three = part // ny
    halfway = width // 2
    for shift in range(ny):
        low = lax.rem(at_y + shift, ny) * three
        count = width // part
        for j in range(count):
            piece[j * three : (j + 1) * three] = turned[pl.ds(pl.multiple_of(j * part + low, 8), three), :]
        for j in range(2):
            piece[(count + j) * three : (count + j + 1) * three] = out_acc[
                pl.ds(pl.multiple_of(low, 8), three), j * halfway : (j + 1) * halfway
            ]
        outs[shift][...] = piece[...].astype(BF16)


def weight_grads(place, sent, packs, ny, after):
    _, rows, width = packs[0].shape
    part = len(sent) * HEAD
    height = (width // part + 2) * (part // ny)
    whole = pl.BlockSpec(memory_space=pltpu.VMEM)
    out = jax.ShapeDtypeStruct((height, 3 * PAD), BF16)
    return pl.pallas_call(
        weights_kernel,
        in_specs=[pl.BlockSpec(memory_space=pltpu.SMEM)]
        + [whole] * (len(sent) + len(packs))
        + [pl.BlockSpec(memory_space=pl.ANY)],
        out_specs=[whole] * ny,
        out_shape=[out] * ny,
        scratch_shapes=[
            pltpu.VMEM((width, 3 * PAD), F32),
            pltpu.VMEM((part, width), F32),
            pltpu.VMEM((height, 3 * PAD), F32),
        ],
        compiler_params=pltpu.CompilerParams(vmem_limit_bytes=VMEM_LIMIT),
        cost_estimate=cost(6),
        name="weight_grads",
    )(place, *sent, *packs, after)


def attention_kernel(scale, place, *refs):
    own_refs, twin_ref, bias_refs, send_ref, pair_refs = refs[:4], refs[4], refs[5:9], refs[9], refs[10:14]
    bias, pair, kt, vt, k_all, v_all, qt, gt, dk_acc, dv_acc = refs[14:]
    step = pl.program_id(0)
    at_x, at_zh, at_y, at_c = place[0], place[1], place[2], place[4]
    nx = len(own_refs)
    rows = twin_ref.shape[2]
    wide = bias.shape[0] // rows
    ny = len(bias_refs)
    chunk = rows // ny
    total = kt.shape[2]
    block = wide * rows
    spots = []
    for x in range(wide):
        for shift in range(ny):
            start = x * rows + lax.rem(at_y + shift, ny) * chunk
            spots.append((x, shift, pl.ds(pl.multiple_of(start, chunk), chunk)))

    @pl.when(step == 0)
    def _():
        for ref in (kt, vt, qt, gt, dk_acc, dv_acc):
            ref[...] = jnp.zeros_like(ref)
        for t in range(2):
            for shift in range(nx):
                slot = lax.rem(at_x + nx - shift, nx)
                own = pl.ds(pl.multiple_of((slot * 2 + at_zh) * rows, rows), rows)
                other = pl.ds(pl.multiple_of((slot * 2 + 1 - at_zh) * rows, rows), rows)
                here = pl.ds(pl.multiple_of(slot * rows, rows), rows)
                for kind, (ref, lanes) in enumerate(
                    ((qt, here), (kt, own), (vt, own), (gt, here), (kt, other), (vt, other))
                ):
                    low = kind * HEAD
                    if t == 0:
                        ref[t, :HEAD, lanes] = own_refs[shift][at_c, low : low + HEAD, :]
                    else:
                        ref[t, :HEAD, lanes] = twin_ref[shift, low : low + HEAD, :]
            k_all[t] = kt[t].T
            v_all[t] = vt[t].T

    for x, shift, spot in spots:
        bias[spot, :] = bias_refs[shift][x]
    lanes = pl.ds(pl.multiple_of(step * block, block), block)
    for t in range(2):
        s = lax.rem(at_c + t, 2)
        q_t, g_t = qt[t, :, lanes], gt[t, :, lanes]
        scores = jnp.dot(q_t.T, kt[t], preferred_element_type=F32) * scale + bias[...].astype(F32)
        peak = jnp.max(scores, axis=-1, keepdims=True)
        expo = jnp.exp(scores - peak)
        probs = expo * (1.0 / jnp.sum(expo, axis=-1, keepdims=True))
        probs_b = probs.astype(BF16)
        att = jnp.dot(probs_b, v_all[t], preferred_element_type=F32).T
        grad_prob = jnp.dot(g_t.T, vt[t], preferred_element_type=F32)
        centre = jnp.sum(probs * grad_prob, axis=-1, keepdims=True)
        grad_score = probs * (grad_prob - centre)
        score_b = grad_score.astype(BF16)
        if t == 0:
            pair[...] = grad_score
        else:
            pair[...] += grad_score
        dq = (jnp.dot(score_b, k_all[t], preferred_element_type=F32) * scale).T
        dk_acc[t] += jnp.dot(q_t, score_b, preferred_element_type=F32)
        dv_acc[t] += jnp.dot(g_t, probs_b, preferred_element_type=F32)
        for x in range(wide):
            send_ref[step * wide + x, s, :HEAD] = att[:HEAD, x * rows : (x + 1) * rows].astype(BF16)
            send_ref[step * wide + x, s, HEAD : 2 * HEAD] = dq[:HEAD, x * rows : (x + 1) * rows].astype(BF16)
    for x, shift, spot in spots:
        pair_refs[shift][x] = pair[spot, :].astype(BF16)

    @pl.when(step == pl.num_programs(0) - 1)
    def _():
        for t in range(2):
            s = lax.rem(at_c + t, 2)
            for at in range(total // rows):
                x, zh = at // 2, at % 2
                low = (2 + 2 * zh) * HEAD
                part = slice(at * rows, (at + 1) * rows)
                send_ref[x, s, low : low + HEAD] = (dk_acc[t, :HEAD, part] * scale).astype(BF16)
                send_ref[x, s, low + HEAD : low + 2 * HEAD] = dv_acc[t, :HEAD, part].astype(BF16)


def attention(head, place, own, twin, bias, scale):
    nx, chunk, total = bias[0].shape
    rows = twin.shape[2]
    wide = 2
    block = wide * rows
    own_spec = pl.BlockSpec((2, 6 * HEAD, rows), lambda i: (0, head, 0))
    twin_spec = pl.BlockSpec((nx, 6 * HEAD, rows), lambda i: (0, head, 0))
    bias_spec = pl.BlockSpec((wide, chunk, total), lambda i: (i, 0, 0))
    pair_shape = jax.ShapeDtypeStruct(bias[0].shape, BF16)
    return pl.pallas_call(
        lambda *refs: attention_kernel(scale, *refs),
        grid=(nx // wide,),
        in_specs=[pl.BlockSpec(memory_space=pltpu.SMEM)] + [own_spec] * 4 + [twin_spec] + [bias_spec] * 4,
        out_specs=[pl.BlockSpec((nx, 2, 6 * HEAD, rows), lambda i: (0, 0, 0, 0))] + [bias_spec] * 4,
        out_shape=[jax.ShapeDtypeStruct((nx, 2, 6 * HEAD, rows), BF16)] + [pair_shape] * 4,
        scratch_shapes=[
            pltpu.VMEM((block, total), BF16),
            pltpu.VMEM((block, total), F32),
            pltpu.VMEM((2, PAD, total), BF16),
            pltpu.VMEM((2, PAD, total), BF16),
            pltpu.VMEM((2, total, PAD), BF16),
            pltpu.VMEM((2, total, PAD), BF16),
            pltpu.VMEM((2, PAD, nx * rows), BF16),
            pltpu.VMEM((2, PAD, nx * rows), BF16),
            pltpu.VMEM((2, PAD, total), F32),
            pltpu.VMEM((2, PAD, total), F32),
        ],
        compiler_params=pltpu.CompilerParams(vmem_limit_bytes=VMEM_LIMIT),
        cost_estimate=cost(9),
        name="attention",
    )(place, *own, twin, *bias)


def exchange(values, axes):
    return lax.all_to_all(values, axes, split_axis=0, concat_axis=0, tiled=True)


def ring(n, shift):
    return [(i, (i + shift) % n) for i in range(n)]


def around(values, axis):
    n = lax.axis_size(axis)
    return [values] + [lax.ppermute(values, axis, ring(n, -shift)) for shift in range(1, n)]


def ring_scatter(pieces, axis):
    n = lax.axis_size(axis)
    total = pieces[0].astype(F32)
    for shift in range(1, n):
        total = total + lax.ppermute(pieces[shift], axis, ring(n, shift)).astype(F32)
    return total


def per_device(activations, pair_bias, w_qkv, w_out, cotangent):
    act = activations[0]
    cot = cotangent[0]
    rows, width = act.shape
    nx, nzh, ny, nzl, nc = (lax.axis_size(a) for a in AXES)
    place = jnp.stack([lax.axis_index(a) for a in AXES]).astype(jnp.int32)
    at_x, at_zh, at_c = place[0], place[1], place[4]
    groups = nx * nc
    heads = H // groups
    part = width // groups
    scale = 1.0 / math.sqrt(HEAD)
    total = pair_bias.shape[2]
    own_rows = pair_bias.shape[1]
    chunk = nzl * nc * own_rows
    swap = [(0, 1), (1, 0)]

    with jax.named_scope("project"):
        act_other = lax.ppermute(act, "zh", swap)
        blocks = project(place, act, act_other, cot, w_qkv, w_out, nx, nc)
        own = [blocks[0]] + [lax.ppermute(blocks[i], "x", ring(nx, i)) for i in range(1, nx)]
        twin = jnp.stack([lax.dynamic_index_in_dim(v, 1 - at_c, 0, keepdims=False) for v in own])
        twin = lax.ppermute(twin, "c", swap)

    with jax.named_scope("bias_in"):
        send = pair_bias.reshape(nx, 1, nc, heads, own_rows, total)
        send = jnp.broadcast_to(send, (nx, nzl, nc, heads, own_rows, total))
        got = exchange(send.reshape(nx * nzl * nc, heads, own_rows, total), ("x", "zl", "c"))
        got = got.reshape(nx, nzl * nc, heads, own_rows, total)
        bias = [around(got[:, :, h].reshape(nx, chunk, total), "y") for h in range(heads)]

    with jax.named_scope("gather"):
        packs = around(pack(act, act_other, cot, own[1:]), "x")
        packs = packs + [lax.ppermute(piece, "c", swap) for piece in packs]

    sent = []
    pairs_out = []
    with jax.named_scope("attention"):
        for h in range(heads):
            out, *pair = attention(h, place, own, twin, bias[h], scale)
            sent.append(out)
            pairs_out.append(pair)

    with jax.named_scope("along_y"):
        sums = [ring_scatter(pair, "y").astype(BF16) for pair in pairs_out]

    with jax.named_scope("weights"):
        weight_pieces = weight_grads(place, sent, packs, ny, sums[0])

    with jax.named_scope("along_y"):
        sums = [v.reshape(nx * nzl * nc, own_rows, total) for v in sums]
        weight_sum = ring_scatter(weight_pieces, "y").astype(BF16)

    with jax.named_scope("owners"):
        three = width // (nx * nzh * ny * nzl * nc)
        cut = nx * nzh * nzl * nc * three
        qkv_part = weight_sum[:cut].reshape(nx, nzh, nzl, nc, three, 3 * PAD).transpose(0, 2, 3, 1, 4, 5)
        out_part = weight_sum[cut:].reshape(1, 2, nzl, nc, three, width // 2).transpose(0, 2, 3, 1, 4, 5)
        here = (jnp.arange(nx) == at_x).reshape(nx, 1, 1, 1, 1, 1)
        out_part = jnp.where(here, out_part, jnp.zeros_like(out_part))
        peers = nx * nzl * nc
        weight_send = jnp.concatenate(
            [qkv_part.reshape(peers, -1), out_part.reshape(peers, -1)], axis=1
        ).reshape(peers, heads * own_rows, -1)
        pair_send = jnp.concatenate(sums, axis=1)
        got = exchange(jnp.concatenate([pair_send, weight_send], axis=2), ("x", "zl", "c"))
        pair_got = got[:, :, :total].reshape(nx, nzl, nc, heads, own_rows, total).astype(F32)
        grad_pair = jnp.sum(pair_got, axis=1).astype(BF16).reshape(H, own_rows, total)
        weight_got = jnp.sum(got[:, :, total:].reshape(nx, nzl, nc, -1).astype(F32), axis=1)
        cut = nzh * three * 3 * PAD
        qkv_part = weight_got[:, :, :cut].reshape(groups, nzh, three, 3, PAD)[..., :part]
        qkv_part = qkv_part.transpose(1, 2, 3, 0, 4).reshape(nzh, three, 3 * width)
        out_part = jnp.sum(weight_got[:, :, cut:], axis=0).reshape(nzh, 2, three, width // 2)
        out_part = out_part.transpose(0, 2, 1, 3).reshape(nzh, three, width)
        partial = jnp.concatenate([qkv_part, out_part], axis=2)
        away = lax.dynamic_index_in_dim(partial, 1 - at_zh, 0, keepdims=False).astype(BF16)
        grad_weights = lax.dynamic_index_in_dim(partial, at_zh, 0, keepdims=False)
        grad_weights = grad_weights + lax.ppermute(away, "zh", swap).astype(F32)

    with jax.named_scope("tokens_out"):
        got = [exchange(v.reshape(groups, 6 * HEAD, rows), ("x", "c")) for v in sent]
        got = jnp.stack(got, axis=1).reshape(groups, heads, 6, HEAD, rows)
        attended = got[:, :, 0].reshape(width, rows)
        grad_query = got[:, :, 1].reshape(width, rows)
        grad_kv = got[:, :, 2:].reshape(groups, heads, nzh, 2, HEAD, rows).transpose(2, 3, 0, 1, 4, 5)
        grad_kv = grad_kv.reshape(nzh, 2 * width, rows)
        kv_own = lax.dynamic_index_in_dim(grad_kv, at_zh, 0, keepdims=False)
        kv_other = lax.dynamic_index_in_dim(grad_kv, 1 - at_zh, 0, keepdims=False)

        def product(left, right, dims):
            return lax.dot_general(left, right, (dims, ((), ())), preferred_element_type=F32)

        grad_other = product(kv_other, w_qkv[:, width:], ((0,), (1,))).astype(BF16)
        grad_other = lax.ppermute(grad_other, "zh", swap)
        update = product(attended, w_out, ((0,), (0,))).astype(BF16)
        grad_own = product(jnp.concatenate([grad_query, kv_own], axis=0), w_qkv, ((0,), (1,)))
        normed, inverse = layer_norm(act.astype(F32))
        grad_act = norm_backward(grad_own + grad_other.astype(F32), normed, inverse).astype(BF16)

    return (update[None], grad_act[None], grad_pair, grad_weights)


def solution(mesh):
    fine = Mesh(mesh.devices.reshape(4, 2, 4, 4, 2), AXES)
    row, samp = ("x", "zh"), ("y", "zl", "c")
    in_specs = (
        P(samp, row, None),
        P(None, row + samp, None),
        P(),
        P(),
        P(samp, row, None),
    )
    out_specs = (
        P(samp, row, None),
        P(samp, row, None),
        P(None, row + samp, None),
        P(row + samp, None),
    )
    return jax.shard_map(
        per_device, mesh=fine, in_specs=in_specs, out_specs=out_specs, check_vma=False
    )
```

```python
import math

import jax
import jax.numpy as jnp
from jax import lax
from jax.experimental import pallas as pl
from jax.experimental.pallas import tpu as pltpu
from jax.sharding import Mesh, PartitionSpec as P

H = 16
HEAD = 48
PAD = 128
AXES = ("x", "zh", "y", "zl", "c")
VMEM_LIMIT = 56 * 1024 * 1024

epsilon = 1e-05
F32 = jnp.float32
BF16 = jnp.bfloat16


def layer_norm(values):
    mean_value = jnp.mean(values, axis=-1, keepdims=True)
    centred = values - mean_value
    variance = jnp.mean(centred * centred, axis=-1, keepdims=True)
    inverse = lax.rsqrt(variance + epsilon)
    return (centred * inverse, inverse)


def norm_backward(grad_in, normed, inverse):
    first_mean = jnp.mean(grad_in, axis=-1, keepdims=True)
    second_mean = jnp.mean(grad_in * normed, axis=-1, keepdims=True)
    return inverse * (grad_in - first_mean - normed * second_mean)


def right_transposed(left, right):
    return lax.dot_general(left, right, (((1,), (1,)), ((), ())), preferred_element_type=F32)


def normalise(values):
    mean_value = jnp.mean(values, axis=-1, keepdims=True)
    centred = values - mean_value
    variance = jnp.mean(centred * centred, axis=-1, keepdims=True)
    return (centred * lax.rsqrt(variance + epsilon)).astype(BF16)


def cost(us):
    return pl.CostEstimate(flops=int(us * 1e9), bytes_accessed=int(us * 3e6), transcendentals=0)


def normed_kernel(act, cot, out):
    out[0] = normalise(act[...].astype(F32))
    out[1] = cot[...]


def pack_rows(act, cot):
    whole = pl.BlockSpec(memory_space=pltpu.VMEM)
    return pl.pallas_call(
        normed_kernel,
        in_specs=[whole] * 2,
        out_specs=whole,
        out_shape=jax.ShapeDtypeStruct((2,) + act.shape, BF16),
        cost_estimate=cost(1),
        name="pack_rows",
    )(act, cot)


def own_kernel(rows, w_qkv, w_out, out):
    width = w_out.shape[0]
    out[: 3 * width] = jnp.dot(rows[0], w_qkv[...], preferred_element_type=F32).T.astype(BF16)
    out[3 * width :] = right_transposed(rows[1], w_out[...]).T.astype(BF16)


def project_own(rows, w_qkv, w_out):
    _, count, width = rows.shape
    whole = pl.BlockSpec(memory_space=pltpu.VMEM)
    return pl.pallas_call(
        own_kernel,
        in_specs=[whole] * 3,
        out_specs=whole,
        out_shape=jax.ShapeDtypeStruct((4 * width, count), BF16),
        compiler_params=pltpu.CompilerParams(vmem_limit_bytes=VMEM_LIMIT),
        cost_estimate=cost(4),
        name="project_own",
    )(rows, w_qkv, w_out)


def project_kernel(place, other, mine, w_qkv, *refs):
    normed_out, outs, turned = refs[0], refs[1:-1], refs[-1]
    at_x = place[0]
    nx, copies = len(outs), normed_out.shape[0]
    rows, width = other.shape
    far = normalise(other[...].astype(F32))
    for i in range(copies):
        normed_out[i] = far
    turned[...] = jnp.dot(far, w_qkv[:, width:], preferred_element_type=F32).T.astype(BF16)
    cores, height, _ = outs[0].shape
    kinds = 6
    heads = height // (kinds * HEAD)
    for shift in range(nx):
        slot = lax.rem(at_x + shift, nx)
        for core in range(cores):
            for h in range(heads):
                for kind in range(kinds):
                    source, at = (mine, kind) if kind < 4 else (turned, kind - 4)
                    start = at * width + ((slot * cores + core) * heads + h) * HEAD
                    row = (h * kinds + kind) * HEAD
                    outs[shift][core, row : row + HEAD] = source[pl.ds(pl.multiple_of(start, 16), HEAD), :]


def project(place, other, mine, w_qkv, nx, nc):
    rows, width = other.shape
    kinds = 6
    whole = pl.BlockSpec(memory_space=pltpu.VMEM)
    out = jax.ShapeDtypeStruct((nc, kinds * width // (nx * nc), rows), BF16)
    return pl.pallas_call(
        project_kernel,
        in_specs=[pl.BlockSpec(memory_space=pltpu.SMEM)] + [whole] * 3,
        out_specs=[whole] * (nx + 1),
        out_shape=[jax.ShapeDtypeStruct((nx, rows, width), BF16)] + [out] * nx,
        scratch_shapes=[pltpu.VMEM((2 * width, rows), BF16)],
        compiler_params=pltpu.CompilerParams(vmem_limit_bytes=VMEM_LIMIT),
        cost_estimate=cost(3),
        name="project",
    )(place, other, mine, w_qkv)


def twin_kernel(place, *refs):
    pieces, out = refs[:4], refs[-1]
    for i, piece in enumerate(pieces):
        out[i] = piece[1 - place[4]]


def for_twin(place, pieces, after):
    whole = pl.BlockSpec(memory_space=pltpu.VMEM)
    return pl.pallas_call(
        twin_kernel,
        in_specs=[pl.BlockSpec(memory_space=pltpu.SMEM)]
        + [whole] * len(pieces)
        + [pl.BlockSpec(memory_space=pl.ANY)] * len(after),
        out_specs=whole,
        out_shape=jax.ShapeDtypeStruct((len(pieces),) + pieces[0].shape[1:], BF16),
        compiler_params=pltpu.CompilerParams(vmem_limit_bytes=VMEM_LIMIT),
        cost_estimate=cost(1),
        name="for_twin",
    )(place, *pieces, *after)


def weights_kernel(place, *refs):
    sent, packs, others, outs, (turned, out_acc, piece) = refs[:2], refs[2:10], refs[10:12], refs[13:17], refs[17:]
    at_x, at_zh, at_y, at_c = place[0], place[1], place[2], place[4]
    heads = len(sent)
    nx = sent[0].shape[0]
    width = packs[0].shape[-1]
    ny = len(outs)
    sums = [None] * 3

    def stacked(x, s, slots):
        return jnp.concatenate(
            [
                sent[h][x, s, pl.ds(pl.multiple_of(slot * HEAD, 16), HEAD), :]
                for slot in slots
                for h in range(heads)
            ],
            axis=0,
        )

    for twin in range(2):
        s = lax.rem(at_c + twin, 2)
        slots = [lax.rem(at_x + shift, nx) for shift in range(nx)]
        pieces = packs[twin * nx : (twin + 1) * nx]
        own, other = 2 + 2 * at_zh, 4 - 2 * at_zh
        kv_left = jnp.concatenate(
            [stacked(x, s, (own, own + 1)) for x in slots] + [stacked(x, s, (other, other + 1)) for x in slots],
            axis=1,
        )
        q_left = jnp.concatenate([stacked(x, s, (1,)) for x in slots], axis=1)
        out_left = jnp.concatenate([stacked(x, s, (0,)) for x in slots], axis=1)
        own_right = jnp.concatenate([p[0] for p in pieces], axis=0)
        other_right = jnp.concatenate([others[twin][x] for x in slots], axis=0)
        out_right = jnp.concatenate([p[1] for p in pieces], axis=0)
        terms = (
            jnp.dot(q_left, own_right, preferred_element_type=F32),
            jnp.dot(kv_left, jnp.concatenate([own_right, other_right], axis=0), preferred_element_type=F32),
            jnp.dot(out_left, out_right, preferred_element_type=F32),
        )
        sums = [t if a is None else a + t for a, t in zip(sums, terms)]
    part = heads * HEAD
    blank = jnp.zeros((PAD - part, width), F32)
    for kind, block in enumerate((sums[0], sums[1][:part], sums[1][part:])):
        turned[:, kind * PAD : (kind + 1) * PAD] = jnp.concatenate([block, blank], axis=0).T
    out_acc[...] = sums[2]
    three = part // ny
    halfway = width // 2
    for shift in range(ny):
        low = lax.rem(at_y + shift, ny) * three
        count = width // part
        for j in range(count):
            piece[j * three : (j + 1) * three] = turned[pl.ds(pl.multiple_of(j * part + low, 8), three), :]
        for j in range(2):
            piece[(count + j) * three : (count + j + 1) * three] = out_acc[
                pl.ds(pl.multiple_of(low, 8), three), j * halfway : (j + 1) * halfway
            ]
        outs[shift][...] = piece[...].astype(BF16)


def weight_grads(place, sent, packs, others, ny, after):
    _, rows, width = packs[0].shape
    part = len(sent) * HEAD
    height = (width // part + 2) * (part // ny)
    whole = pl.BlockSpec(memory_space=pltpu.VMEM)
    out = jax.ShapeDtypeStruct((height, 3 * PAD), BF16)
    return pl.pallas_call(
        weights_kernel,
        in_specs=[pl.BlockSpec(memory_space=pltpu.SMEM)]
        + [whole] * (len(sent) + len(packs) + len(others))
        + [pl.BlockSpec(memory_space=pl.ANY)],
        out_specs=[whole] * ny,
        out_shape=[out] * ny,
        scratch_shapes=[
            pltpu.VMEM((width, 3 * PAD), F32),
            pltpu.VMEM((part, width), F32),
            pltpu.VMEM((height, 3 * PAD), F32),
        ],
        compiler_params=pltpu.CompilerParams(vmem_limit_bytes=VMEM_LIMIT),
        cost_estimate=cost(6),
        name="weight_grads",
    )(place, *sent, *packs, *others, after)


def attention_kernel(scale, place, *refs):
    own_refs, twin_ref, bias_refs, send_ref, pair_refs = refs[:4], refs[4], refs[5:9], refs[9], refs[10:14]
    bias, pair, kt, vt, k_all, v_all, qt, gt, dk_acc, dv_acc = refs[14:]
    step = pl.program_id(0)
    at_x, at_zh, at_y, at_c = place[0], place[1], place[2], place[4]
    nx = len(own_refs)
    rows = twin_ref.shape[2]
    wide = bias.shape[0] // rows
    ny = len(bias_refs)
    chunk = rows // ny
    total = kt.shape[2]
    block = wide * rows
    spots = []
    for x in range(wide):
        for shift in range(ny):
            start = x * rows + lax.rem(at_y + shift, ny) * chunk
            spots.append((x, shift, pl.ds(pl.multiple_of(start, chunk), chunk)))

    @pl.when(step == 0)
    def _():
        for ref in (kt, vt, qt, gt, dk_acc, dv_acc):
            ref[...] = jnp.zeros_like(ref)
        for t in range(2):
            for shift in range(nx):
                slot = lax.rem(at_x + nx - shift, nx)
                own = pl.ds(pl.multiple_of((slot * 2 + at_zh) * rows, rows), rows)
                other = pl.ds(pl.multiple_of((slot * 2 + 1 - at_zh) * rows, rows), rows)
                here = pl.ds(pl.multiple_of(slot * rows, rows), rows)
                for kind, (ref, lanes) in enumerate(
                    ((qt, here), (kt, own), (vt, own), (gt, here), (kt, other), (vt, other))
                ):
                    low = kind * HEAD
                    if t == 0:
                        ref[t, :HEAD, lanes] = own_refs[shift][at_c, low : low + HEAD, :]
                    else:
                        ref[t, :HEAD, lanes] = twin_ref[shift, low : low + HEAD, :]
            k_all[t] = kt[t].T
            v_all[t] = vt[t].T

    for x, shift, spot in spots:
        bias[spot, :] = bias_refs[shift][x]
    lanes = pl.ds(pl.multiple_of(step * block, block), block)
    for t in range(2):
        s = lax.rem(at_c + t, 2)
        q_t, g_t = qt[t, :, lanes], gt[t, :, lanes]
        scores = jnp.dot(q_t.T, kt[t], preferred_element_type=F32) * scale + bias[...].astype(F32)
        peak = jnp.max(scores, axis=-1, keepdims=True)
        expo = jnp.exp(scores - peak)
        probs = expo * (1.0 / jnp.sum(expo, axis=-1, keepdims=True))
        probs_b = probs.astype(BF16)
        att = jnp.dot(probs_b, v_all[t], preferred_element_type=F32).T
        grad_prob = jnp.dot(g_t.T, vt[t], preferred_element_type=F32)
        centre = jnp.sum(probs * grad_prob, axis=-1, keepdims=True)
        grad_score = probs * (grad_prob - centre)
        score_b = grad_score.astype(BF16)
        if t == 0:
            pair[...] = grad_score
        else:
            pair[...] += grad_score
        dq = (jnp.dot(score_b, k_all[t], preferred_element_type=F32) * scale).T
        dk_acc[t] += jnp.dot(q_t, score_b, preferred_element_type=F32)
        dv_acc[t] += jnp.dot(g_t, probs_b, preferred_element_type=F32)
        for x in range(wide):
            send_ref[step * wide + x, s, :HEAD] = att[:HEAD, x * rows : (x + 1) * rows].astype(BF16)
            send_ref[step * wide + x, s, HEAD : 2 * HEAD] = dq[:HEAD, x * rows : (x + 1) * rows].astype(BF16)
    for x, shift, spot in spots:
        pair_refs[shift][x] = pair[spot, :].astype(BF16)

    @pl.when(step == pl.num_programs(0) - 1)
    def _():
        for t in range(2):
            s = lax.rem(at_c + t, 2)
            for at in range(total // rows):
                x, zh = at // 2, at % 2
                low = (2 + 2 * zh) * HEAD
                part = slice(at * rows, (at + 1) * rows)
                send_ref[x, s, low : low + HEAD] = (dk_acc[t, :HEAD, part] * scale).astype(BF16)
                send_ref[x, s, low + HEAD : low + 2 * HEAD] = dv_acc[t, :HEAD, part].astype(BF16)


def attention(head, place, own, twin, bias, scale):
    nx, chunk, total = bias[0].shape
    rows = twin.shape[2]
    wide = 2
    block = wide * rows
    own_spec = pl.BlockSpec((2, 6 * HEAD, rows), lambda i: (0, head, 0))
    twin_spec = pl.BlockSpec((nx, 6 * HEAD, rows), lambda i: (0, head, 0))
    bias_spec = pl.BlockSpec((wide, chunk, total), lambda i: (i, 0, 0))
    pair_shape = jax.ShapeDtypeStruct(bias[0].shape, BF16)
    return pl.pallas_call(
        lambda *refs: attention_kernel(scale, *refs),
        grid=(nx // wide,),
        in_specs=[pl.BlockSpec(memory_space=pltpu.SMEM)] + [own_spec] * 4 + [twin_spec] + [bias_spec] * 4,
        out_specs=[pl.BlockSpec((nx, 2, 6 * HEAD, rows), lambda i: (0, 0, 0, 0))] + [bias_spec] * 4,
        out_shape=[jax.ShapeDtypeStruct((nx, 2, 6 * HEAD, rows), BF16)] + [pair_shape] * 4,
        scratch_shapes=[
            pltpu.VMEM((block, total), BF16),
            pltpu.VMEM((block, total), F32),
            pltpu.VMEM((2, PAD, total), BF16),
            pltpu.VMEM((2, PAD, total), BF16),
            pltpu.VMEM((2, total, PAD), BF16),
            pltpu.VMEM((2, total, PAD), BF16),
            pltpu.VMEM((2, PAD, nx * rows), BF16),
            pltpu.VMEM((2, PAD, nx * rows), BF16),
            pltpu.VMEM((2, PAD, total), F32),
            pltpu.VMEM((2, PAD, total), F32),
        ],
        compiler_params=pltpu.CompilerParams(vmem_limit_bytes=VMEM_LIMIT),
        cost_estimate=cost(9),
        name="attention",
    )(place, *own, twin, *bias)


def exchange(values, axes):
    return lax.all_to_all(values, axes, split_axis=0, concat_axis=0, tiled=True)


def ring(n, shift):
    return [(i, (i + shift) % n) for i in range(n)]


def around(values, axis):
    n = lax.axis_size(axis)
    return [values] + [lax.ppermute(values, axis, ring(n, -shift)) for shift in range(1, n)]


def ring_scatter(pieces, axis):
    n = lax.axis_size(axis)
    total = pieces[0].astype(F32)
    for shift in range(1, n):
        total = total + lax.ppermute(pieces[shift], axis, ring(n, shift)).astype(F32)
    return total


def per_device(activations, pair_bias, w_qkv, w_out, cotangent):
    act = activations[0]
    cot = cotangent[0]
    rows, width = act.shape
    nx, nzh, ny, nzl, nc = (lax.axis_size(a) for a in AXES)
    place = jnp.stack([lax.axis_index(a) for a in AXES]).astype(jnp.int32)
    at_x, at_zh, at_c = place[0], place[1], place[4]
    groups = nx * nc
    heads = H // groups
    part = width // groups
    scale = 1.0 / math.sqrt(HEAD)
    total = pair_bias.shape[2]
    own_rows = pair_bias.shape[1]
    chunk = nzl * nc * own_rows
    swap = [(0, 1), (1, 0)]

    with jax.named_scope("gather"):
        act_other = lax.ppermute(act, "zh", swap)
        rows_own = pack_rows(act, cot)
        packs = around(rows_own, "x")

    with jax.named_scope("bias_in"):
        send = pair_bias.reshape(nx, 1, nc, heads, own_rows, total)
        send = jnp.broadcast_to(send, (nx, nzl, nc, heads, own_rows, total))
        got = exchange(send.reshape(nx * nzl * nc, heads, own_rows, total), ("x", "zl", "c"))
        got = got.reshape(nx, nzl * nc, heads, own_rows, total)
        bias = [around(got[:, :, h].reshape(nx, chunk, total), "y") for h in range(heads)]

    with jax.named_scope("project"):
        mine = project_own(rows_own, w_qkv, w_out)
        other_rows, *blocks = project(place, act_other, mine, w_qkv, nx, nc)
        own = [blocks[0]] + [lax.ppermute(blocks[i], "x", ring(nx, i)) for i in range(1, nx)]
        twin = lax.ppermute(for_twin(place, own, [bias[0][0]]), "c", swap)

    with jax.named_scope("gather"):
        packs = packs + [lax.ppermute(piece, "c", swap) for piece in packs]
        other_rows = exchange(other_rows, "x")
        others = [other_rows, lax.ppermute(other_rows, "c", swap)]

    sent = []
    pairs_out = []
    with jax.named_scope("attention"):
        for h in range(heads):
            out, *pair = attention(h, place, own, twin, bias[h], scale)
            sent.append(out)
            pairs_out.append(pair)

    with jax.named_scope("along_y"):
        sums = [ring_scatter(pair, "y").astype(BF16) for pair in pairs_out]

    with jax.named_scope("weights"):
        weight_pieces = weight_grads(place, sent, packs, others, ny, sums[0])

    with jax.named_scope("along_y"):
        sums = [v.reshape(nx * nzl * nc, own_rows, total) for v in sums]
        weight_sum = ring_scatter(weight_pieces, "y").astype(BF16)

    with jax.named_scope("owners"):
        got = exchange(jnp.stack(sums, axis=1), ("x", "zl", "c"))
        got = got.reshape(nx, nzl, nc, heads, own_rows, total).astype(F32)
        grad_pair = jnp.sum(got, axis=1).astype(BF16).reshape(H, own_rows, total)

    with jax.named_scope("weight_owners"):
        at_zl = place[3]
        three = width // (nx * nzh * ny * nzl * nc)
        lanes = 3 * PAD
        cut = nx * nzh * nzl * nc * three
        qkv_part = weight_sum[:cut].reshape(nx * nzh, nzl, nc * three, lanes).transpose(1, 0, 2, 3)
        out_part = weight_sum[cut:].reshape(2, nzl, nc * three, lanes).transpose(1, 0, 2, 3)
        parts = jnp.concatenate([qkv_part, out_part], axis=1)

        def pick(values, at, axis=0):
            return lax.dynamic_index_in_dim(values, at, axis, keepdims=False)

        total_part = pick(parts, at_zl).astype(F32)
        for k in range(1, nzl):
            perm = [(i, i ^ k) for i in range(nzl)]
            total_part = total_part + lax.ppermute(pick(parts, at_zl ^ k), "zl", perm).astype(F32)
        qkv_part = total_part[: nx * nzh].reshape(nx, nzh, nc * three, lanes)
        out_part = total_part[nx * nzh :]
        away = jnp.concatenate([pick(qkv_part, 1 - at_zh, 1), out_part], axis=0).astype(BF16)
        got = lax.ppermute(away, "zh", swap).astype(F32)
        part_sum = jnp.concatenate([pick(qkv_part, at_zh, 1), out_part], axis=0) + got
        part_sum = part_sum.reshape(nx + 2, nc, three, lanes).astype(BF16)
        got = lax.ppermute(pick(part_sum, 1 - at_c, 1), "c", swap)
        kept = pick(part_sum, at_c, 1)
        out_part = jnp.where(at_zh == at_c, kept[nx:], got[nx:]).transpose(1, 0, 2).reshape(three, width)
        first = jnp.where(at_c == 0, kept[:nx], got[:nx])
        second = jnp.where(at_c == 0, got[:nx], kept[:nx])
        blocks = jnp.stack([first, second], axis=1)
        arrived = jnp.stack(
            [pick(blocks, at_x)]
            + [lax.ppermute(pick(blocks, (at_x + k) % nx), "x", ring(nx, k)) for k in range(1, nx)]
        )
        arrived = jnp.stack([pick(arrived, (at_x - i) % nx) for i in range(nx)])
        qkv_part = arrived.reshape(groups, three, 3, PAD)[..., :part].transpose(1, 2, 0, 3)
        grad_weights = jnp.concatenate([qkv_part.reshape(three, 3 * width), out_part], axis=1).astype(F32)

    with jax.named_scope("tokens_out"):
        got = [exchange(v.reshape(groups, 6 * HEAD, rows), ("x", "c")) for v in sent]
        got = jnp.stack(got, axis=1).reshape(groups, heads, 6, HEAD, rows)
        attended = got[:, :, 0].reshape(width, rows)
        grad_query = got[:, :, 1].reshape(width, rows)
        grad_kv = got[:, :, 2:].reshape(groups, heads, nzh, 2, HEAD, rows).transpose(2, 3, 0, 1, 4, 5)
        grad_kv = grad_kv.reshape(nzh, 2 * width, rows)
        kv_own = lax.dynamic_index_in_dim(grad_kv, at_zh, 0, keepdims=False)
        kv_other = lax.dynamic_index_in_dim(grad_kv, 1 - at_zh, 0, keepdims=False)

        def product(left, right, dims):
            return lax.dot_general(left, right, (dims, ((), ())), preferred_element_type=F32)

        grad_other = product(kv_other, w_qkv[:, width:], ((0,), (1,))).astype(BF16)
        grad_other = lax.ppermute(grad_other, "zh", swap)
        update = product(attended, w_out, ((0,), (0,))).astype(BF16)
        grad_own = product(jnp.concatenate([grad_query, kv_own], axis=0), w_qkv, ((0,), (1,)))
        normed, inverse = layer_norm(act.astype(F32))
        grad_act = norm_backward(grad_own + grad_other.astype(F32), normed, inverse).astype(BF16)

    return (update[None], grad_act[None], grad_pair, grad_weights)


def solution(mesh):
    fine = Mesh(mesh.devices.reshape(4, 2, 4, 4, 2), AXES)
    row, samp = ("x", "zh"), ("y", "zl", "c")
    in_specs = (
        P(samp, row, None),
        P(None, row + samp, None),
        P(),
        P(),
        P(samp, row, None),
    )
    out_specs = (
        P(samp, row, None),
        P(samp, row, None),
        P(None, row + samp, None),
        P(row + samp, None),
    )
    return jax.shard_map(
        per_device, mesh=fine, in_specs=in_specs, out_specs=out_specs, check_vma=False
    )
```

```python
import math

import jax
import jax.numpy as jnp
from jax import lax
from jax.experimental import pallas as pl
from jax.experimental.pallas import tpu as pltpu
from jax.sharding import Mesh, PartitionSpec as P

H = 16
HEAD = 48
PAD = 128
AXES = ("x", "zh", "y", "zl", "c")
VMEM_LIMIT = 56 * 1024 * 1024

epsilon = 1e-05
F32 = jnp.float32
BF16 = jnp.bfloat16


def layer_norm(values):
    mean_value = jnp.mean(values, axis=-1, keepdims=True)
    centred = values - mean_value
    variance = jnp.mean(centred * centred, axis=-1, keepdims=True)
    inverse = lax.rsqrt(variance + epsilon)
    return (centred * inverse, inverse)


def norm_backward(grad_in, normed, inverse):
    first_mean = jnp.mean(grad_in, axis=-1, keepdims=True)
    second_mean = jnp.mean(grad_in * normed, axis=-1, keepdims=True)
    return inverse * (grad_in - first_mean - normed * second_mean)


def right_transposed(left, right):
    return lax.dot_general(left, right, (((1,), (1,)), ((), ())), preferred_element_type=F32)


def normalise(values):
    mean_value = jnp.mean(values, axis=-1, keepdims=True)
    centred = values - mean_value
    variance = jnp.mean(centred * centred, axis=-1, keepdims=True)
    return (centred * lax.rsqrt(variance + epsilon)).astype(BF16)


def cost(us):
    return pl.CostEstimate(flops=int(us * 1e9), bytes_accessed=int(us * 3e6), transcendentals=0)


def select_heads(window, offset):
    source = lax.broadcasted_iota(jnp.int32, (window.shape[1], PAD), 0)
    target = lax.broadcasted_iota(jnp.int32, (window.shape[1], PAD), 1)
    chosen = ((source == offset + target) & (target < 2 * HEAD)).astype(F32).astype(BF16)
    return jnp.dot(window, chosen, preferred_element_type=F32).astype(BF16)


def columns_kernel(place, w_qkv, w_out, columns, rows):
    width = w_out.shape[0]
    part = 2 * HEAD
    first = (place[0] * 2 + place[4]) * part
    start = jnp.minimum(lax.div(first, PAD) * PAD, width - 2 * PAD)
    for kind in range(3):
        lanes = pl.ds(pl.multiple_of(kind * width + start, PAD), 2 * PAD)
        columns[:, kind * PAD : (kind + 1) * PAD] = select_heads(w_qkv[:, lanes], first - start)
    own = w_out[pl.ds(pl.multiple_of(first, 16), part), :]
    rows[...] = jnp.concatenate([own, jnp.zeros((PAD - part, width), BF16)], axis=0).T


def own_columns(place, w_qkv, w_out):
    width = w_out.shape[0]
    whole = pl.BlockSpec(memory_space=pltpu.VMEM)
    return pl.pallas_call(
        columns_kernel,
        in_specs=[pl.BlockSpec(memory_space=pltpu.SMEM)] + [whole] * 2,
        out_specs=[whole] * 2,
        out_shape=[
            jax.ShapeDtypeStruct((width, 3 * PAD), BF16),
            jax.ShapeDtypeStruct((width, PAD), BF16),
        ],
        compiler_params=pltpu.CompilerParams(vmem_limit_bytes=VMEM_LIMIT),
        cost_estimate=cost(2),
        name="own_columns",
    )(place, w_qkv, w_out)


def project_kernel(number, *refs):
    pieces, twins, columns, rows = refs[:number], refs[number : 2 * number], refs[2 * number], refs[2 * number + 1]
    normed, outs = refs[-2 * number : -number], refs[-number:]
    count = pieces[0].shape[1]
    kinds = outs[0].shape[1] // (2 * HEAD)
    parts = [[], []]
    cots = []
    for i in range(number):
        for t, ref in enumerate((pieces[i], twins[i])):
            for part in range(2):
                value = normalise(ref[part].astype(F32))
                normed[i][t, part] = value
                parts[part].append(value)
            cots.append(ref[2])
    own = jnp.dot(jnp.concatenate(parts[0], axis=0), columns[...], preferred_element_type=F32)
    far = jnp.dot(jnp.concatenate(parts[1], axis=0), columns[:, PAD:], preferred_element_type=F32)
    grads = jnp.dot(jnp.concatenate(cots, axis=0), rows[...], preferred_element_type=F32)
    blocks = [own[:, :PAD], own[:, PAD : 2 * PAD], own[:, 2 * PAD :], grads, far[:, :PAD], far[:, PAD:]]
    for i in range(number):
        for t in range(2):
            for kind, block in enumerate(blocks):
                at = (2 * i + t) * count
                turned = block[at : at + count].T.astype(BF16)
                for h in range(2):
                    low = (h * kinds + kind) * HEAD
                    outs[i][t, low : low + HEAD] = turned[h * HEAD : (h + 1) * HEAD]


def project(pieces, twins, columns, rows):
    number = len(pieces)
    _, count, width = pieces[0].shape
    whole = pl.BlockSpec(memory_space=pltpu.VMEM)
    return pl.pallas_call(
        lambda *refs: project_kernel(number, *refs),
        in_specs=[whole] * (2 * number + 2),
        out_specs=[whole] * (2 * number),
        out_shape=[jax.ShapeDtypeStruct((2, 2, count, width), BF16)] * number
        + [jax.ShapeDtypeStruct((2, 12 * HEAD, count), BF16)] * number,
        compiler_params=pltpu.CompilerParams(vmem_limit_bytes=VMEM_LIMIT),
        cost_estimate=cost(2 * number),
        name="project",
    )(*pieces, *twins, columns, rows)


def gate(values, *after):
    away = pl.BlockSpec(memory_space=pl.ANY)
    return pl.pallas_call(
        lambda *refs: None,
        in_specs=[away] * (1 + len(after)),
        out_specs=away,
        out_shape=jax.ShapeDtypeStruct(values.shape, values.dtype),
        input_output_aliases={0: 0},
        cost_estimate=cost(0.1),
        name="gate",
    )(values, *after)


def weights_kernel(place, sent, *refs):
    outs, (turned, out_acc, piece) = refs[-7:-3], refs[-3:]
    at_x, at_zh, at_y, at_c = place[0], place[1], place[2], place[4]
    nx, _, heads, _, _ = sent.shape
    normed, cots = refs[:nx], refs[nx : 3 * nx]
    width = normed[0].shape[-1]
    ny = len(outs)
    sums = [None] * 3

    def stacked(x, s, slots):
        return jnp.concatenate(
            [
                sent[x, s, h, pl.ds(pl.multiple_of(slot * HEAD, 16), HEAD), :]
                for slot in slots
                for h in range(heads)
            ],
            axis=0,
        )

    order = [lax.rem(at_x + shift, nx) for shift in range(nx)]
    for twin in range(2):
        s = lax.rem(at_c + twin, 2)
        own, other = 2 + 2 * at_zh, 4 - 2 * at_zh
        kv_left = jnp.concatenate(
            [stacked(x, s, (own, own + 1)) for x in order]
            + [stacked(x, s, (other, other + 1)) for x in order],
            axis=1,
        )
        q_left = jnp.concatenate([stacked(x, s, (1,)) for x in order], axis=1)
        out_left = jnp.concatenate([stacked(x, s, (0,)) for x in order], axis=1)
        own_right = jnp.concatenate([p[twin, 0] for p in normed], axis=0)
        other_right = jnp.concatenate([p[twin, 1] for p in normed], axis=0)
        out_right = jnp.concatenate([p[0] for p in cots[twin * nx : (twin + 1) * nx]], axis=0)
        terms = (
            jnp.dot(q_left, own_right, preferred_element_type=F32),
            jnp.dot(kv_left, jnp.concatenate([own_right, other_right], axis=0), preferred_element_type=F32),
            jnp.dot(out_left, out_right, preferred_element_type=F32),
        )
        sums = [t if a is None else a + t for a, t in zip(sums, terms)]
    part = heads * HEAD
    blank = jnp.zeros((PAD - part, width), F32)
    for kind, block in enumerate((sums[0], sums[1][:part], sums[1][part:])):
        turned[:, kind * PAD : (kind + 1) * PAD] = jnp.concatenate([block, blank], axis=0).T
    out_acc[...] = sums[2]
    three = part // ny
    halfway = width // 2
    for shift in range(ny):
        low = lax.rem(at_y + shift, ny) * three
        count = width // part
        for j in range(count):
            piece[j * three : (j + 1) * three] = turned[pl.ds(pl.multiple_of(j * part + low, 8), three), :]
        for j in range(2):
            piece[(count + j) * three : (count + j + 1) * three] = out_acc[
                pl.ds(pl.multiple_of(low, 8), three), j * halfway : (j + 1) * halfway
            ]
        outs[shift][...] = piece[...].astype(BF16)


def weight_grads(place, sent, normed, pieces, ny, after):
    heads, rows = sent.shape[2], sent.shape[4]
    width = normed[0].shape[-1]
    part = heads * HEAD
    height = (width // part + 2) * (part // ny)
    whole = lambda a: pl.BlockSpec(a.shape, lambda i: (0,) * a.ndim)
    cot_spec = pl.BlockSpec((1, rows, width), lambda i: (2, 0, 0))
    out = jax.ShapeDtypeStruct((height, 3 * PAD), BF16)
    return pl.pallas_call(
        weights_kernel,
        grid=(1,),
        in_specs=[pl.BlockSpec(memory_space=pltpu.SMEM), whole(sent)]
        + [whole(v) for v in normed]
        + [cot_spec] * len(pieces)
        + [pl.BlockSpec(memory_space=pl.ANY)] * len(after),
        out_specs=[pl.BlockSpec(out.shape, lambda i: (0, 0))] * ny,
        out_shape=[out] * ny,
        scratch_shapes=[
            pltpu.VMEM((width, 3 * PAD), F32),
            pltpu.VMEM((part, width), F32),
            pltpu.VMEM((height, 3 * PAD), F32),
        ],
        compiler_params=pltpu.CompilerParams(vmem_limit_bytes=VMEM_LIMIT),
        cost_estimate=cost(6),
        name="weight_grads",
    )(place, sent, *normed, *pieces, *after)


def attention_kernel(scale, place, *refs):
    own_refs, bias_refs, send_ref, pair_refs = refs[:4], refs[4:8], refs[-15], refs[-14:-10]
    bias, pair, kt, vt, k_all, v_all, qt, gt, dk_acc, dv_acc = refs[-10:]
    step = pl.program_id(0)
    at_x, at_zh, at_y, at_c = place[0], place[1], place[2], place[4]
    nx = len(own_refs)
    rows = own_refs[0].shape[2]
    wide = bias.shape[0] // rows
    ny = len(bias_refs)
    chunk = rows // ny
    total = kt.shape[2]
    block = wide * rows
    spots = []
    for x in range(wide):
        for shift in range(ny):
            start = x * rows + lax.rem(at_y + shift, ny) * chunk
            spots.append((x, shift, pl.ds(pl.multiple_of(start, chunk), chunk)))

    @pl.when(step == 0)
    def _():
        for ref in (kt, vt, qt, gt, dk_acc, dv_acc):
            ref[...] = jnp.zeros_like(ref)
        for t in range(2):
            for shift in range(nx):
                slot = lax.rem(at_x + shift, nx)
                own = pl.ds(pl.multiple_of((slot * 2 + at_zh) * rows, rows), rows)
                other = pl.ds(pl.multiple_of((slot * 2 + 1 - at_zh) * rows, rows), rows)
                here = pl.ds(pl.multiple_of(slot * rows, rows), rows)
                for kind, (ref, lanes) in enumerate(
                    ((qt, here), (kt, own), (vt, own), (gt, here), (kt, other), (vt, other))
                ):
                    low = kind * HEAD
                    ref[t, :HEAD, lanes] = own_refs[shift][t, low : low + HEAD, :]
            k_all[t] = kt[t].T
            v_all[t] = vt[t].T

    for x, shift, spot in spots:
        bias[spot, :] = bias_refs[shift][x]
    lanes = pl.ds(pl.multiple_of(step * block, block), block)
    for t in range(2):
        s = lax.rem(at_c + t, 2)
        q_t, g_t = qt[t, :, lanes], gt[t, :, lanes]
        scores = jnp.dot(q_t.T, kt[t], preferred_element_type=F32) * scale + bias[...].astype(F32)
        peak = jnp.max(scores, axis=-1, keepdims=True)
        expo = jnp.exp(scores - peak)
        probs = expo * (1.0 / jnp.sum(expo, axis=-1, keepdims=True))
        probs_b = probs.astype(BF16)
        att = jnp.dot(probs_b, v_all[t], preferred_element_type=F32).T
        grad_prob = jnp.dot(g_t.T, vt[t], preferred_element_type=F32)
        centre = jnp.sum(probs * grad_prob, axis=-1, keepdims=True)
        grad_score = probs * (grad_prob - centre)
        score_b = grad_score.astype(BF16)
        if t == 0:
            pair[...] = grad_score
        else:
            pair[...] += grad_score
        dq = (jnp.dot(score_b, k_all[t], preferred_element_type=F32) * scale).T
        dk_acc[t] += jnp.dot(q_t, score_b, preferred_element_type=F32)
        dv_acc[t] += jnp.dot(g_t, probs_b, preferred_element_type=F32)
        for x in range(wide):
            send_ref[step * wide + x, s, 0, :HEAD] = att[:HEAD, x * rows : (x + 1) * rows].astype(BF16)
            send_ref[step * wide + x, s, 0, HEAD : 2 * HEAD] = dq[:HEAD, x * rows : (x + 1) * rows].astype(BF16)
    for x, shift, spot in spots:
        pair_refs[shift][x] = pair[spot, :].astype(BF16)

    @pl.when(step == pl.num_programs(0) - 1)
    def _():
        for t in range(2):
            s = lax.rem(at_c + t, 2)
            for at in range(total // rows):
                x, zh = at // 2, at % 2
                low = (2 + 2 * zh) * HEAD
                part = slice(at * rows, (at + 1) * rows)
                send_ref[x, s, 0, low : low + HEAD] = (dk_acc[t, :HEAD, part] * scale).astype(BF16)
                send_ref[x, s, 0, low + HEAD : low + 2 * HEAD] = dv_acc[t, :HEAD, part].astype(BF16)


def attention(head, heads, place, own, bias, sent, scale):
    nx, chunk, total = bias[0].shape
    rows = own[0].shape[2]
    wide = 2
    block = wide * rows
    own_spec = pl.BlockSpec((2, 6 * HEAD, rows), lambda i: (0, head, 0))
    bias_spec = pl.BlockSpec((wide, chunk, total), lambda i: (i, 0, 0))
    pair_shape = jax.ShapeDtypeStruct(bias[0].shape, BF16)
    return pl.pallas_call(
        lambda *refs: attention_kernel(scale, *refs),
        grid=(nx // wide,),
        in_specs=[pl.BlockSpec(memory_space=pltpu.SMEM)]
        + [own_spec] * 4
        + [bias_spec] * 4
        + [pl.BlockSpec(memory_space=pl.ANY)] * len(sent),
        out_specs=[pl.BlockSpec((nx, 2, 1, 6 * HEAD, rows), lambda i: (0, 0, head, 0, 0))] + [bias_spec] * 4,
        out_shape=[jax.ShapeDtypeStruct((nx, 2, heads, 6 * HEAD, rows), BF16)] + [pair_shape] * 4,
        input_output_aliases={9 + i: i for i in range(len(sent))},
        scratch_shapes=[
            pltpu.VMEM((block, total), BF16),
            pltpu.VMEM((block, total), F32),
            pltpu.VMEM((2, PAD, total), BF16),
            pltpu.VMEM((2, PAD, total), BF16),
            pltpu.VMEM((2, total, PAD), BF16),
            pltpu.VMEM((2, total, PAD), BF16),
            pltpu.VMEM((2, PAD, nx * rows), BF16),
            pltpu.VMEM((2, PAD, nx * rows), BF16),
            pltpu.VMEM((2, PAD, total), F32),
            pltpu.VMEM((2, PAD, total), F32),
        ],
        compiler_params=pltpu.CompilerParams(vmem_limit_bytes=VMEM_LIMIT),
        cost_estimate=cost(9),
        name="attention",
    )(place, *own, *bias, *sent)


def exchange(values, axes):
    return lax.all_to_all(values, axes, split_axis=0, concat_axis=0, tiled=True)


def ring(n, shift):
    return [(i, (i + shift) % n) for i in range(n)]


def around(values, axis):
    n = lax.axis_size(axis)
    return [values] + [lax.ppermute(values, axis, ring(n, -shift)) for shift in range(1, n)]


def ring_scatter(pieces, axis):
    n = lax.axis_size(axis)
    return [lax.ppermute(pieces[shift], axis, ring(n, shift)) for shift in range(1, n)]


def added(own, got):
    total = own.astype(F32)
    for piece in got:
        total = total + piece.astype(F32)
    return total


def per_device(activations, pair_bias, w_qkv, w_out, cotangent):
    act = activations[0]
    cot = cotangent[0]
    rows, width = act.shape
    nx, nzh, ny, nzl, nc = (lax.axis_size(a) for a in AXES)
    place = jnp.stack([lax.axis_index(a) for a in AXES]).astype(jnp.int32)
    at_x, at_zh, at_c = place[0], place[1], place[4]
    groups = nx * nc
    heads = H // groups
    part = width // groups
    scale = 1.0 / math.sqrt(HEAD)
    total = pair_bias.shape[2]
    own_rows = pair_bias.shape[1]
    chunk = nzl * nc * own_rows
    swap = [(0, 1), (1, 0)]

    with jax.named_scope("rows_in"):
        act_other = lax.ppermute(act, "zh", swap)
        columns, rows_out = own_columns(place, w_qkv, w_out)
        pieces = around(jnp.stack([act, act_other, cot]), "x")
        twin = lax.ppermute(pieces[0], "c", swap)

    with jax.named_scope("project"):
        first = project(pieces[:1], [twin], columns, rows_out)

    with jax.named_scope("bias_in"):
        send = pair_bias.reshape(nx, 1, nc, heads, own_rows, total)
        send = jnp.broadcast_to(send, (nx, nzl, nc, heads, own_rows, total))
        got = exchange(send.reshape(nx * nzl * nc, heads, own_rows, total), ("x", "zl", "c"))
        got = gate(got, first[1]).reshape(nx, nzl * nc, heads, own_rows, total)
        bias = [around(got[:, :, h].reshape(nx, chunk, total), "y") for h in range(heads)]

    with jax.named_scope("project"):
        ready = [first[1], bias[0][0], bias[1][0]]
        ready = [[], ready, bias[0][1:], ready]
        pieces = pieces[:1] + [gate(pieces[i], *ready[i]) for i in range(1, nx)]
        twins = [twin] + [lax.ppermute(piece, "c", swap) for piece in pieces[1:]]
        later = project(pieces[1:], twins[1:], columns, rows_out)
        normed = first[:1] + later[: nx - 1]
        own = first[1:] + later[nx - 1 :]

    sent = []
    pairs_out = []
    with jax.named_scope("attention"):
        for h in range(heads):
            out, *pair = attention(h, heads, place, own, bias[h], sent, scale)
            sent = [out]
            pairs_out.append(pair)

    with jax.named_scope("along_y"):
        arrived = [ring_scatter(pair, "y") for pair in pairs_out]
        sums = [added(pair[0], got) for pair, got in zip(pairs_out, arrived)]
        sums = [v.astype(BF16).reshape(nx * nzl * nc, own_rows, total) for v in sums]

    with jax.named_scope("weights"):
        weight_pieces = weight_grads(place, sent[0], normed, pieces + twins, ny, arrived[0][:1])

    with jax.named_scope("along_y"):
        weight_sum = added(weight_pieces[0], ring_scatter(weight_pieces, "y")).astype(BF16)

    with jax.named_scope("owners"):
        three = width // (nx * nzh * ny * nzl * nc)
        cut = nx * nzh * nzl * nc * three
        qkv_part = weight_sum[:cut].reshape(nx, nzh, nzl, nc, three, 3 * PAD).transpose(0, 2, 3, 1, 4, 5)
        out_part = weight_sum[cut:].reshape(1, 2, nzl, nc, three, width // 2).transpose(0, 2, 3, 1, 4, 5)
        here = (jnp.arange(nx) == at_x).reshape(nx, 1, 1, 1, 1, 1)
        out_part = jnp.where(here, out_part, jnp.zeros_like(out_part))
        peers = nx * nzl * nc
        weight_send = jnp.concatenate(
            [qkv_part.reshape(peers, -1), out_part.reshape(peers, -1)], axis=1
        ).reshape(peers, heads * own_rows, -1)
        pair_send = jnp.concatenate(sums, axis=1)
        got = exchange(jnp.concatenate([pair_send, weight_send], axis=2), ("x", "zl", "c"))
        pair_got = got[:, :, :total].reshape(nx, nzl, nc, heads, own_rows, total).astype(F32)
        grad_pair = jnp.sum(pair_got, axis=1).astype(BF16).reshape(H, own_rows, total)
        weight_got = jnp.sum(got[:, :, total:].reshape(nx, nzl, nc, -1).astype(F32), axis=1)
        cut = nzh * three * 3 * PAD
        qkv_part = weight_got[:, :, :cut].reshape(groups, nzh, three, 3, PAD)[..., :part]
        qkv_part = qkv_part.transpose(1, 2, 3, 0, 4).reshape(nzh, three, 3 * width)
        out_part = jnp.sum(weight_got[:, :, cut:], axis=0).reshape(nzh, 2, three, width // 2)
        out_part = out_part.transpose(0, 2, 1, 3).reshape(nzh, three, width)
        partial = jnp.concatenate([qkv_part, out_part], axis=2)
        away = lax.dynamic_index_in_dim(partial, 1 - at_zh, 0, keepdims=False).astype(BF16)
        grad_weights = lax.dynamic_index_in_dim(partial, at_zh, 0, keepdims=False)
        grad_weights = grad_weights + lax.ppermute(away, "zh", swap).astype(F32)

    with jax.named_scope("tokens_out"):
        got = exchange(sent[0].reshape(groups, heads * 6 * HEAD, rows), ("x", "c"))
        got = got.reshape(groups, heads, 6, HEAD, rows)
        attended = got[:, :, 0].reshape(width, rows)
        grad_query = got[:, :, 1].reshape(width, rows)
        grad_kv = got[:, :, 2:].reshape(groups, heads, nzh, 2, HEAD, rows).transpose(2, 3, 0, 1, 4, 5)
        grad_kv = grad_kv.reshape(nzh, 2 * width, rows)
        kv_own = lax.dynamic_index_in_dim(grad_kv, at_zh, 0, keepdims=False)
        kv_other = lax.dynamic_index_in_dim(grad_kv, 1 - at_zh, 0, keepdims=False)

        def product(left, right, dims):
            return lax.dot_general(left, right, (dims, ((), ())), preferred_element_type=F32)

        grad_other = product(kv_other, w_qkv[:, width:], ((0,), (1,))).astype(BF16)
        grad_other = lax.ppermute(grad_other, "zh", swap)
        update = product(attended, w_out, ((0,), (0,))).astype(BF16)
        grad_own = product(jnp.concatenate([grad_query, kv_own], axis=0), w_qkv, ((0,), (1,)))
        normed, inverse = layer_norm(act.astype(F32))
        grad_act = norm_backward(grad_own + grad_other.astype(F32), normed, inverse).astype(BF16)

    return (update[None], grad_act[None], grad_pair, grad_weights)


def solution(mesh):
    fine = Mesh(mesh.devices.reshape(4, 2, 4, 4, 2), AXES)
    row, samp = ("x", "zh"), ("y", "zl", "c")
    in_specs = (
        P(samp, row, None),
        P(None, row + samp, None),
        P(),
        P(),
        P(samp, row, None),
    )
    out_specs = (
        P(samp, row, None),
        P(samp, row, None),
        P(None, row + samp, None),
        P(row + samp, None),
    )
    return jax.shard_map(
        per_device, mesh=fine, in_specs=in_specs, out_specs=out_specs, check_vma=False
    )
```

```python
import math

import jax
import jax.numpy as jnp
from jax import lax
from jax.experimental import pallas as pl
from jax.experimental.pallas import tpu as pltpu
from jax.sharding import Mesh, PartitionSpec as P

H = 16
HEAD = 48
PAD = 128
AXES = ("x", "zh", "y", "zl", "c")
VMEM_LIMIT = 56 * 1024 * 1024

epsilon = 1e-05
F32 = jnp.float32
BF16 = jnp.bfloat16


def layer_norm(values):
    mean_value = jnp.mean(values, axis=-1, keepdims=True)
    centred = values - mean_value
    variance = jnp.mean(centred * centred, axis=-1, keepdims=True)
    inverse = lax.rsqrt(variance + epsilon)
    return (centred * inverse, inverse)


def norm_backward(grad_in, normed, inverse):
    first_mean = jnp.mean(grad_in, axis=-1, keepdims=True)
    second_mean = jnp.mean(grad_in * normed, axis=-1, keepdims=True)
    return inverse * (grad_in - first_mean - normed * second_mean)


def right_transposed(left, right):
    return lax.dot_general(left, right, (((1,), (1,)), ((), ())), preferred_element_type=F32)


def normalise(values):
    mean_value = jnp.mean(values, axis=-1, keepdims=True)
    centred = values - mean_value
    variance = jnp.mean(centred * centred, axis=-1, keepdims=True)
    return (centred * lax.rsqrt(variance + epsilon)).astype(BF16)


def cost(us):
    return pl.CostEstimate(flops=int(us * 1e9), bytes_accessed=int(us * 3e6), transcendentals=0)


def select_heads(window, offset):
    source = lax.broadcasted_iota(jnp.int32, (window.shape[1], PAD), 0)
    target = lax.broadcasted_iota(jnp.int32, (window.shape[1], PAD), 1)
    chosen = ((source == offset + target) & (target < 2 * HEAD)).astype(F32).astype(BF16)
    return jnp.dot(window, chosen, preferred_element_type=F32).astype(BF16)


def columns_kernel(place, w_qkv, w_out, columns, rows):
    width = w_out.shape[0]
    part = 2 * HEAD
    first = (place[0] * 2 + place[4]) * part
    start = jnp.minimum(lax.div(first, PAD) * PAD, width - 2 * PAD)
    for kind in range(3):
        lanes = pl.ds(pl.multiple_of(kind * width + start, PAD), 2 * PAD)
        columns[:, kind * PAD : (kind + 1) * PAD] = select_heads(w_qkv[:, lanes], first - start)
    own = w_out[pl.ds(pl.multiple_of(first, 16), part), :]
    rows[...] = jnp.concatenate([own, jnp.zeros((PAD - part, width), BF16)], axis=0).T


def own_columns(place, w_qkv, w_out):
    width = w_out.shape[0]
    whole = pl.BlockSpec(memory_space=pltpu.VMEM)
    return pl.pallas_call(
        columns_kernel,
        in_specs=[pl.BlockSpec(memory_space=pltpu.SMEM)] + [whole] * 2,
        out_specs=[whole] * 2,
        out_shape=[
            jax.ShapeDtypeStruct((width, 3 * PAD), BF16),
            jax.ShapeDtypeStruct((width, PAD), BF16),
        ],
        compiler_params=pltpu.CompilerParams(vmem_limit_bytes=VMEM_LIMIT),
        cost_estimate=cost(2),
        name="own_columns",
    )(place, w_qkv, w_out)


def project_kernel(number, *refs):
    pieces, twins, columns, rows = refs[:number], refs[number : 2 * number], refs[2 * number], refs[2 * number + 1]
    normed, outs = refs[-2 * number : -number], refs[-number:]
    count = pieces[0].shape[1]
    kinds = outs[0].shape[1] // (2 * HEAD)
    parts = [[], []]
    cots = []
    for i in range(number):
        for t, ref in enumerate((pieces[i], twins[i])):
            for part in range(2):
                value = normalise(ref[part].astype(F32))
                normed[i][t, part] = value
                parts[part].append(value)
            cots.append(ref[2])
    own = jnp.dot(jnp.concatenate(parts[0], axis=0), columns[...], preferred_element_type=F32)
    far = jnp.dot(jnp.concatenate(parts[1], axis=0), columns[:, PAD:], preferred_element_type=F32)
    grads = jnp.dot(jnp.concatenate(cots, axis=0), rows[...], preferred_element_type=F32)
    blocks = [own[:, :PAD], own[:, PAD : 2 * PAD], own[:, 2 * PAD :], grads, far[:, :PAD], far[:, PAD:]]
    for i in range(number):
        for t in range(2):
            for kind, block in enumerate(blocks):
                at = (2 * i + t) * count
                turned = block[at : at + count].T.astype(BF16)
                for h in range(2):
                    low = (h * kinds + kind) * HEAD
                    outs[i][t, low : low + HEAD] = turned[h * HEAD : (h + 1) * HEAD]


def project(pieces, twins, columns, rows):
    number = len(pieces)
    _, count, width = pieces[0].shape
    whole = pl.BlockSpec(memory_space=pltpu.VMEM)
    return pl.pallas_call(
        lambda *refs: project_kernel(number, *refs),
        in_specs=[whole] * (2 * number + 2),
        out_specs=[whole] * (2 * number),
        out_shape=[jax.ShapeDtypeStruct((2, 2, count, width), BF16)] * number
        + [jax.ShapeDtypeStruct((2, 12 * HEAD, count), BF16)] * number,
        compiler_params=pltpu.CompilerParams(vmem_limit_bytes=VMEM_LIMIT),
        cost_estimate=cost(2 * number),
        name="project",
    )(*pieces, *twins, columns, rows)


def gate(values, *after):
    away = pl.BlockSpec(memory_space=pl.ANY)
    return pl.pallas_call(
        lambda *refs: None,
        in_specs=[away] * (1 + len(after)),
        out_specs=away,
        out_shape=jax.ShapeDtypeStruct(values.shape, values.dtype),
        input_output_aliases={0: 0},
        cost_estimate=cost(0.1),
        name="gate",
    )(values, *after)


def weights_kernel(place, sent, *refs):
    outs, (turned, out_acc, piece) = refs[-7:-3], refs[-3:]
    at_x, at_zh, at_y, at_c = place[0], place[1], place[2], place[4]
    nx, _, heads, _, _ = sent.shape
    normed, cots = refs[:nx], refs[nx : 3 * nx]
    width = normed[0].shape[-1]
    ny = len(outs)
    sums = [None] * 3

    def stacked(x, s, slots):
        return jnp.concatenate(
            [
                sent[x, s, h, pl.ds(pl.multiple_of(slot * HEAD, 16), HEAD), :]
                for slot in slots
                for h in range(heads)
            ],
            axis=0,
        )

    order = [lax.rem(at_x + shift, nx) for shift in range(nx)]
    for twin in range(2):
        s = lax.rem(at_c + twin, 2)
        own, other = 2 + 2 * at_zh, 4 - 2 * at_zh
        kv_left = jnp.concatenate(
            [stacked(x, s, (own, own + 1)) for x in order]
            + [stacked(x, s, (other, other + 1)) for x in order],
            axis=1,
        )
        q_left = jnp.concatenate([stacked(x, s, (1,)) for x in order], axis=1)
        out_left = jnp.concatenate([stacked(x, s, (0,)) for x in order], axis=1)
        own_right = jnp.concatenate([p[twin, 0] for p in normed], axis=0)
        other_right = jnp.concatenate([p[twin, 1] for p in normed], axis=0)
        out_right = jnp.concatenate([p[0] for p in cots[twin * nx : (twin + 1) * nx]], axis=0)
        terms = (
            jnp.dot(q_left, own_right, preferred_element_type=F32),
            jnp.dot(kv_left, jnp.concatenate([own_right, other_right], axis=0), preferred_element_type=F32),
            jnp.dot(out_left, out_right, preferred_element_type=F32),
        )
        sums = [t if a is None else a + t for a, t in zip(sums, terms)]
    part = heads * HEAD
    blank = jnp.zeros((PAD - part, width), F32)
    for kind, block in enumerate((sums[0], sums[1][:part], sums[1][part:])):
        turned[:, kind * PAD : (kind + 1) * PAD] = jnp.concatenate([block, blank], axis=0).T
    out_acc[...] = sums[2]
    three = part // ny
    halfway = width // 2
    for shift in range(ny):
        low = lax.rem(at_y + shift, ny) * three
        count = width // part
        for j in range(count):
            piece[j * three : (j + 1) * three] = turned[pl.ds(pl.multiple_of(j * part + low, 8), three), :]
        for j in range(2):
            piece[(count + j) * three : (count + j + 1) * three] = out_acc[
                pl.ds(pl.multiple_of(low, 8), three), j * halfway : (j + 1) * halfway
            ]
        outs[shift][...] = piece[...].astype(BF16)


def weight_grads(place, sent, normed, pieces, ny, after):
    heads, rows = sent.shape[2], sent.shape[4]
    width = normed[0].shape[-1]
    part = heads * HEAD
    height = (width // part + 2) * (part // ny)
    whole = lambda a: pl.BlockSpec(a.shape, lambda i: (0,) * a.ndim)
    cot_spec = pl.BlockSpec((1, rows, width), lambda i: (2, 0, 0))
    out = jax.ShapeDtypeStruct((height, 3 * PAD), BF16)
    return pl.pallas_call(
        weights_kernel,
        grid=(1,),
        in_specs=[pl.BlockSpec(memory_space=pltpu.SMEM), whole(sent)]
        + [whole(v) for v in normed]
        + [cot_spec] * len(pieces)
        + [pl.BlockSpec(memory_space=pl.ANY)] * len(after),
        out_specs=[pl.BlockSpec(out.shape, lambda i: (0, 0))] * ny,
        out_shape=[out] * ny,
        scratch_shapes=[
            pltpu.VMEM((width, 3 * PAD), F32),
            pltpu.VMEM((part, width), F32),
            pltpu.VMEM((height, 3 * PAD), F32),
        ],
        compiler_params=pltpu.CompilerParams(vmem_limit_bytes=VMEM_LIMIT),
        cost_estimate=cost(6),
        name="weight_grads",
    )(place, sent, *normed, *pieces, *after)


def attention_kernel(scale, place, *refs):
    own_refs, bias_refs, send_ref, pair_refs = refs[:4], refs[4:8], refs[-15], refs[-14:-10]
    bias, pair, kt, vt, k_all, v_all, qt, gt, dk_acc, dv_acc = refs[-10:]
    step = pl.program_id(0)
    at_x, at_zh, at_y, at_c = place[0], place[1], place[2], place[4]
    nx = len(own_refs)
    rows = own_refs[0].shape[2]
    wide = bias.shape[0] // rows
    ny = len(bias_refs)
    chunk = rows // ny
    total = kt.shape[2]
    block = wide * rows
    spots = []
    for x in range(wide):
        for shift in range(ny):
            start = x * rows + lax.rem(at_y + shift, ny) * chunk
            spots.append((x, shift, pl.ds(pl.multiple_of(start, chunk), chunk)))

    @pl.when(step == 0)
    def _():
        for ref in (kt, vt, qt, gt, dk_acc, dv_acc):
            ref[...] = jnp.zeros_like(ref)
        for t in range(2):
            for shift in range(nx):
                slot = lax.rem(at_x + shift, nx)
                own = pl.ds(pl.multiple_of((slot * 2 + at_zh) * rows, rows), rows)
                other = pl.ds(pl.multiple_of((slot * 2 + 1 - at_zh) * rows, rows), rows)
                here = pl.ds(pl.multiple_of(slot * rows, rows), rows)
                for kind, (ref, lanes) in enumerate(
                    ((qt, here), (kt, own), (vt, own), (gt, here), (kt, other), (vt, other))
                ):
                    low = kind * HEAD
                    ref[t, :HEAD, lanes] = own_refs[shift][t, low : low + HEAD, :]
            k_all[t] = kt[t].T
            v_all[t] = vt[t].T

    for x, shift, spot in spots:
        bias[spot, :] = bias_refs[shift][x]
    lanes = pl.ds(pl.multiple_of(step * block, block), block)
    for t in range(2):
        s = lax.rem(at_c + t, 2)
        q_t, g_t = qt[t, :, lanes], gt[t, :, lanes]
        scores = jnp.dot(q_t.T, kt[t], preferred_element_type=F32) * scale + bias[...].astype(F32)
        peak = jnp.max(scores, axis=-1, keepdims=True)
        expo = jnp.exp(scores - peak)
        probs = expo * (1.0 / jnp.sum(expo, axis=-1, keepdims=True))
        probs_b = probs.astype(BF16)
        att = jnp.dot(probs_b, v_all[t], preferred_element_type=F32).T
        grad_prob = jnp.dot(g_t.T, vt[t], preferred_element_type=F32)
        centre = jnp.sum(probs * grad_prob, axis=-1, keepdims=True)
        grad_score = probs * (grad_prob - centre)
        score_b = grad_score.astype(BF16)
        if t == 0:
            pair[...] = grad_score
        else:
            pair[...] += grad_score
        dq = (jnp.dot(score_b, k_all[t], preferred_element_type=F32) * scale).T
        dk_acc[t] += jnp.dot(q_t, score_b, preferred_element_type=F32)
        dv_acc[t] += jnp.dot(g_t, probs_b, preferred_element_type=F32)
        for x in range(wide):
            send_ref[step * wide + x, s, 0, :HEAD] = att[:HEAD, x * rows : (x + 1) * rows].astype(BF16)
            send_ref[step * wide + x, s, 0, HEAD : 2 * HEAD] = dq[:HEAD, x * rows : (x + 1) * rows].astype(BF16)
    for x, shift, spot in spots:
        pair_refs[shift][x] = pair[spot, :].astype(BF16)

    @pl.when(step == pl.num_programs(0) - 1)
    def _():
        for t in range(2):
            s = lax.rem(at_c + t, 2)
            for at in range(total // rows):
                x, zh = at // 2, at % 2
                low = (2 + 2 * zh) * HEAD
                part = slice(at * rows, (at + 1) * rows)
                send_ref[x, s, 0, low : low + HEAD] = (dk_acc[t, :HEAD, part] * scale).astype(BF16)
                send_ref[x, s, 0, low + HEAD : low + 2 * HEAD] = dv_acc[t, :HEAD, part].astype(BF16)


def attention(head, heads, place, own, bias, sent, scale):
    nx, chunk, total = bias[0].shape
    rows = own[0].shape[2]
    wide = 2
    block = wide * rows
    own_spec = pl.BlockSpec((2, 6 * HEAD, rows), lambda i: (0, head, 0))
    bias_spec = pl.BlockSpec((wide, chunk, total), lambda i: (i, 0, 0))
    pair_shape = jax.ShapeDtypeStruct(bias[0].shape, BF16)
    return pl.pallas_call(
        lambda *refs: attention_kernel(scale, *refs),
        grid=(nx // wide,),
        in_specs=[pl.BlockSpec(memory_space=pltpu.SMEM)]
        + [own_spec] * 4
        + [bias_spec] * 4
        + [pl.BlockSpec(memory_space=pl.ANY)] * len(sent),
        out_specs=[pl.BlockSpec((nx, 2, 1, 6 * HEAD, rows), lambda i: (0, 0, head, 0, 0))] + [bias_spec] * 4,
        out_shape=[jax.ShapeDtypeStruct((nx, 2, heads, 6 * HEAD, rows), BF16)] + [pair_shape] * 4,
        input_output_aliases={9 + i: i for i in range(len(sent))},
        scratch_shapes=[
            pltpu.VMEM((block, total), BF16),
            pltpu.VMEM((block, total), F32),
            pltpu.VMEM((2, PAD, total), BF16),
            pltpu.VMEM((2, PAD, total), BF16),
            pltpu.VMEM((2, total, PAD), BF16),
            pltpu.VMEM((2, total, PAD), BF16),
            pltpu.VMEM((2, PAD, nx * rows), BF16),
            pltpu.VMEM((2, PAD, nx * rows), BF16),
            pltpu.VMEM((2, PAD, total), F32),
            pltpu.VMEM((2, PAD, total), F32),
        ],
        compiler_params=pltpu.CompilerParams(vmem_limit_bytes=VMEM_LIMIT),
        cost_estimate=cost(9),
        name="attention",
    )(place, *own, *bias, *sent)


def exchange(values, axes):
    return lax.all_to_all(values, axes, split_axis=0, concat_axis=0, tiled=True)


def ring(n, shift):
    return [(i, (i + shift) % n) for i in range(n)]


def around(values, axis):
    n = lax.axis_size(axis)
    return [values] + [lax.ppermute(values, axis, ring(n, -shift)) for shift in range(1, n)]


def ring_scatter(pieces, axis):
    n = lax.axis_size(axis)
    return [lax.ppermute(pieces[shift], axis, ring(n, shift)) for shift in range(1, n)]


def added(own, got):
    total = own.astype(F32)
    for piece in got:
        total = total + piece.astype(F32)
    return total


def per_device(activations, pair_bias, w_qkv, w_out, cotangent):
    act = activations[0]
    cot = cotangent[0]
    rows, width = act.shape
    nx, nzh, ny, nzl, nc = (lax.axis_size(a) for a in AXES)
    place = jnp.stack([lax.axis_index(a) for a in AXES]).astype(jnp.int32)
    at_x, at_zh, at_c = place[0], place[1], place[4]
    groups = nx * nc
    heads = H // groups
    part = width // groups
    scale = 1.0 / math.sqrt(HEAD)
    total = pair_bias.shape[2]
    own_rows = pair_bias.shape[1]
    chunk = nzl * nc * own_rows
    swap = [(0, 1), (1, 0)]

    with jax.named_scope("rows_in"):
        act_other = lax.ppermute(act, "zh", swap)
        columns, rows_out = own_columns(place, w_qkv, w_out)
        pieces = around(jnp.stack([act, act_other, cot]), "x")
        twin = lax.ppermute(pieces[0], "c", swap)

    with jax.named_scope("project"):
        first = project(pieces[:1], [twin], columns, rows_out)

    with jax.named_scope("bias_in"):
        send = pair_bias.reshape(nx, 1, nc, heads, own_rows, total)
        send = jnp.broadcast_to(send, (nx, nzl, nc, heads, own_rows, total))
        got = exchange(send.reshape(nx * nzl * nc, heads, own_rows, total), ("x", "zl", "c"))
        got = gate(got, first[1]).reshape(nx, nzl * nc, heads, own_rows, total)
        bias = [around(got[:, :, h].reshape(nx, chunk, total), "y") for h in range(heads)]

    with jax.named_scope("project"):
        pieces = [pieces[0], pieces[1], gate(pieces[2], *bias[0][1:]), pieces[3]]
        twins = [twin] + [lax.ppermute(piece, "c", swap) for piece in pieces[1:]]
        later = project(pieces[1:], twins[1:], columns, rows_out)
        normed = first[:1] + later[: nx - 1]
        own = first[1:] + later[nx - 1 :]

    sent = []
    pairs_out = []
    with jax.named_scope("attention"):
        for h in range(heads):
            out, *pair = attention(h, heads, place, own, bias[h], sent, scale)
            sent = [out]
            pairs_out.append(pair)

    with jax.named_scope("along_y"):
        arrived = [ring_scatter(pair, "y") for pair in pairs_out]
        sums = [added(pair[0], got) for pair, got in zip(pairs_out, arrived)]
        sums = [v.astype(BF16).reshape(nx * nzl * nc, own_rows, total) for v in sums]

    with jax.named_scope("weights"):
        weight_pieces = weight_grads(place, sent[0], normed, pieces + twins, ny, arrived[0][:1])

    with jax.named_scope("along_y"):
        weight_sum = added(weight_pieces[0], ring_scatter(weight_pieces, "y")).astype(BF16)

    with jax.named_scope("owners"):
        three = width // (nx * nzh * ny * nzl * nc)
        cut = nx * nzh * nzl * nc * three
        qkv_part = weight_sum[:cut].reshape(nx, nzh, nzl, nc, three, 3 * PAD).transpose(0, 2, 3, 1, 4, 5)
        out_part = weight_sum[cut:].reshape(1, 2, nzl, nc, three, width // 2).transpose(0, 2, 3, 1, 4, 5)
        here = (jnp.arange(nx) == at_x).reshape(nx, 1, 1, 1, 1, 1)
        out_part = jnp.where(here, out_part, jnp.zeros_like(out_part))
        peers = nx * nzl * nc
        weight_send = jnp.concatenate(
            [qkv_part.reshape(peers, -1), out_part.reshape(peers, -1)], axis=1
        ).reshape(peers, heads * own_rows, -1)
        pair_send = jnp.concatenate(sums, axis=1)
        got = exchange(jnp.concatenate([pair_send, weight_send], axis=2), ("x", "zl", "c"))
        pair_got = got[:, :, :total].reshape(nx, nzl, nc, heads, own_rows, total).astype(F32)
        grad_pair = jnp.sum(pair_got, axis=1).astype(BF16).reshape(H, own_rows, total)
        weight_got = jnp.sum(got[:, :, total:].reshape(nx, nzl, nc, -1).astype(F32), axis=1)
        cut = nzh * three * 3 * PAD
        qkv_part = weight_got[:, :, :cut].reshape(groups, nzh, three, 3, PAD)[..., :part]
        qkv_part = qkv_part.transpose(1, 2, 3, 0, 4).reshape(nzh, three, 3 * width)
        out_part = jnp.sum(weight_got[:, :, cut:], axis=0).reshape(nzh, 2, three, width // 2)
        out_part = out_part.transpose(0, 2, 1, 3).reshape(nzh, three, width)
        partial = jnp.concatenate([qkv_part, out_part], axis=2)
        away = lax.dynamic_index_in_dim(partial, 1 - at_zh, 0, keepdims=False).astype(BF16)
        grad_weights = lax.dynamic_index_in_dim(partial, at_zh, 0, keepdims=False)
        grad_weights = grad_weights + lax.ppermute(away, "zh", swap).astype(F32)

    with jax.named_scope("tokens_out"):
        got = exchange(sent[0].reshape(groups, heads * 6 * HEAD, rows), ("x", "c"))
        got = got.reshape(groups, heads, 6, HEAD, rows)
        attended = got[:, :, 0].reshape(width, rows)
        grad_query = got[:, :, 1].reshape(width, rows)
        grad_kv = got[:, :, 2:].reshape(groups, heads, nzh, 2, HEAD, rows).transpose(2, 3, 0, 1, 4, 5)
        grad_kv = grad_kv.reshape(nzh, 2 * width, rows)
        kv_own = lax.dynamic_index_in_dim(grad_kv, at_zh, 0, keepdims=False)
        kv_other = lax.dynamic_index_in_dim(grad_kv, 1 - at_zh, 0, keepdims=False)

        def product(left, right, dims):
            return lax.dot_general(left, right, (dims, ((), ())), preferred_element_type=F32)

        grad_other = product(kv_other, w_qkv[:, width:], ((0,), (1,))).astype(BF16)
        grad_other = lax.ppermute(grad_other, "zh", swap)
        update = product(attended, w_out, ((0,), (0,))).astype(BF16)
        grad_own = product(jnp.concatenate([grad_query, kv_own], axis=0), w_qkv, ((0,), (1,)))
        normed, inverse = layer_norm(act.astype(F32))
        grad_act = norm_backward(grad_own + grad_other.astype(F32), normed, inverse).astype(BF16)

    return (update[None], grad_act[None], grad_pair, grad_weights)


def solution(mesh):
    fine = Mesh(mesh.devices.reshape(4, 2, 4, 4, 2), AXES)
    row, samp = ("x", "zh"), ("y", "zl", "c")
    in_specs = (
        P(samp, row, None),
        P(None, row + samp, None),
        P(),
        P(),
        P(samp, row, None),
    )
    out_specs = (
        P(samp, row, None),
        P(samp, row, None),
        P(None, row + samp, None),
        P(row + samp, None),
    )
    return jax.shard_map(
        per_device, mesh=fine, in_specs=in_specs, out_specs=out_specs, check_vma=False
    )
```

```python
import math

import jax
import jax.numpy as jnp
from jax import lax
from jax.experimental import pallas as pl
from jax.experimental.pallas import tpu as pltpu
from jax.sharding import Mesh, PartitionSpec as P

H = 16
HEAD = 48
PAD = 128
AXES = ("x", "zh", "y", "zl", "c")
VMEM_LIMIT = 56 * 1024 * 1024

epsilon = 1e-05
F32 = jnp.float32
BF16 = jnp.bfloat16


def layer_norm(values):
    mean_value = jnp.mean(values, axis=-1, keepdims=True)
    centred = values - mean_value
    variance = jnp.mean(centred * centred, axis=-1, keepdims=True)
    inverse = lax.rsqrt(variance + epsilon)
    return (centred * inverse, inverse)


def norm_backward(grad_in, normed, inverse):
    first_mean = jnp.mean(grad_in, axis=-1, keepdims=True)
    second_mean = jnp.mean(grad_in * normed, axis=-1, keepdims=True)
    return inverse * (grad_in - first_mean - normed * second_mean)


def right_transposed(left, right):
    return lax.dot_general(left, right, (((1,), (1,)), ((), ())), preferred_element_type=F32)


def normalise(values):
    mean_value = jnp.mean(values, axis=-1, keepdims=True)
    centred = values - mean_value
    variance = jnp.mean(centred * centred, axis=-1, keepdims=True)
    return (centred * lax.rsqrt(variance + epsilon)).astype(BF16)


def cost(us):
    return pl.CostEstimate(flops=int(us * 1e9), bytes_accessed=int(us * 3e6), transcendentals=0)


def select_heads(window, offset):
    source = lax.broadcasted_iota(jnp.int32, (window.shape[1], PAD), 0)
    target = lax.broadcasted_iota(jnp.int32, (window.shape[1], PAD), 1)
    chosen = ((source == offset + target) & (target < 2 * HEAD)).astype(F32).astype(BF16)
    return jnp.dot(window, chosen, preferred_element_type=F32).astype(BF16)


def columns_kernel(place, w_qkv, w_out, columns, rows):
    width = w_out.shape[0]
    part = 2 * HEAD
    first = (place[0] * 2 + place[4]) * part
    start = jnp.minimum(lax.div(first, PAD) * PAD, width - 2 * PAD)
    for kind in range(3):
        lanes = pl.ds(pl.multiple_of(kind * width + start, PAD), 2 * PAD)
        columns[:, kind * PAD : (kind + 1) * PAD] = select_heads(w_qkv[:, lanes], first - start)
    own = w_out[pl.ds(pl.multiple_of(first, 16), part), :]
    rows[...] = jnp.concatenate([own, jnp.zeros((PAD - part, width), BF16)], axis=0).T


def own_columns(place, w_qkv, w_out):
    width = w_out.shape[0]
    whole = pl.BlockSpec(memory_space=pltpu.VMEM)
    return pl.pallas_call(
        columns_kernel,
        in_specs=[pl.BlockSpec(memory_space=pltpu.SMEM)] + [whole] * 2,
        out_specs=[whole] * 2,
        out_shape=[
            jax.ShapeDtypeStruct((width, 3 * PAD), BF16),
            jax.ShapeDtypeStruct((width, PAD), BF16),
        ],
        compiler_params=pltpu.CompilerParams(vmem_limit_bytes=VMEM_LIMIT),
        cost_estimate=cost(2),
        name="own_columns",
    )(place, w_qkv, w_out)


def project_kernel(number, *refs):
    pieces, twins, columns, rows = refs[:number], refs[number : 2 * number], refs[2 * number], refs[2 * number + 1]
    normed, outs = refs[-2 * number : -number], refs[-number:]
    count = pieces[0].shape[1]
    kinds = outs[0].shape[1] // (2 * HEAD)
    parts = [[], []]
    cots = []
    for i in range(number):
        for t, ref in enumerate((pieces[i], twins[i])):
            for part in range(2):
                value = normalise(ref[part].astype(F32))
                normed[i][t, part] = value
                parts[part].append(value)
            cots.append(ref[2])
    own = jnp.dot(jnp.concatenate(parts[0], axis=0), columns[...], preferred_element_type=F32)
    far = jnp.dot(jnp.concatenate(parts[1], axis=0), columns[:, PAD:], preferred_element_type=F32)
    grads = jnp.dot(jnp.concatenate(cots, axis=0), rows[...], preferred_element_type=F32)
    blocks = [own[:, :PAD], own[:, PAD : 2 * PAD], own[:, 2 * PAD :], grads, far[:, :PAD], far[:, PAD:]]
    for i in range(number):
        for t in range(2):
            for kind, block in enumerate(blocks):
                at = (2 * i + t) * count
                turned = block[at : at + count].T.astype(BF16)
                for h in range(2):
                    low = (h * kinds + kind) * HEAD
                    outs[i][t, low : low + HEAD] = turned[h * HEAD : (h + 1) * HEAD]


def project(pieces, twins, columns, rows):
    number = len(pieces)
    _, count, width = pieces[0].shape
    whole = pl.BlockSpec(memory_space=pltpu.VMEM)
    return pl.pallas_call(
        lambda *refs: project_kernel(number, *refs),
        in_specs=[whole] * (2 * number + 2),
        out_specs=[whole] * (2 * number),
        out_shape=[jax.ShapeDtypeStruct((2, 2, count, width), BF16)] * number
        + [jax.ShapeDtypeStruct((2, 12 * HEAD, count), BF16)] * number,
        compiler_params=pltpu.CompilerParams(vmem_limit_bytes=VMEM_LIMIT),
        cost_estimate=cost(2 * number),
        name="project",
    )(*pieces, *twins, columns, rows)


def gate(values, *after):
    away = pl.BlockSpec(memory_space=pl.ANY)
    return pl.pallas_call(
        lambda *refs: None,
        in_specs=[away] * (1 + len(after)),
        out_specs=away,
        out_shape=jax.ShapeDtypeStruct(values.shape, values.dtype),
        input_output_aliases={0: 0},
        cost_estimate=cost(0.1),
        name="gate",
    )(values, *after)


def weights_kernel(place, sent, *refs):
    outs, (turned, out_acc, piece) = refs[-7:-3], refs[-3:]
    at_x, at_zh, at_y, at_c = place[0], place[1], place[2], place[4]
    nx, _, heads, _, _ = sent.shape
    normed, cots = refs[:nx], refs[nx : 3 * nx]
    width = normed[0].shape[-1]
    ny = len(outs)
    sums = [None] * 3

    def stacked(x, s, slots):
        return jnp.concatenate(
            [
                sent[x, s, h, pl.ds(pl.multiple_of(slot * HEAD, 16), HEAD), :]
                for slot in slots
                for h in range(heads)
            ],
            axis=0,
        )

    order = [lax.rem(at_x + shift, nx) for shift in range(nx)]
    for twin in range(2):
        s = lax.rem(at_c + twin, 2)
        own, other = 2 + 2 * at_zh, 4 - 2 * at_zh
        kv_left = jnp.concatenate(
            [stacked(x, s, (own, own + 1)) for x in order]
            + [stacked(x, s, (other, other + 1)) for x in order],
            axis=1,
        )
        q_left = jnp.concatenate([stacked(x, s, (1,)) for x in order], axis=1)
        out_left = jnp.concatenate([stacked(x, s, (0,)) for x in order], axis=1)
        own_right = jnp.concatenate([p[twin, 0] for p in normed], axis=0)
        other_right = jnp.concatenate([p[twin, 1] for p in normed], axis=0)
        out_right = jnp.concatenate([p[0] for p in cots[twin * nx : (twin + 1) * nx]], axis=0)
        terms = (
            jnp.dot(q_left, own_right, preferred_element_type=F32),
            jnp.dot(kv_left, jnp.concatenate([own_right, other_right], axis=0), preferred_element_type=F32),
            jnp.dot(out_left, out_right, preferred_element_type=F32),
        )
        sums = [t if a is None else a + t for a, t in zip(sums, terms)]
    part = heads * HEAD
    blank = jnp.zeros((PAD - part, width), F32)
    for kind, block in enumerate((sums[0], sums[1][:part], sums[1][part:])):
        turned[:, kind * PAD : (kind + 1) * PAD] = jnp.concatenate([block, blank], axis=0).T
    out_acc[...] = sums[2]
    three = part // ny
    halfway = width // 2
    for shift in range(ny):
        low = lax.rem(at_y + shift, ny) * three
        count = width // part
        for j in range(count):
            piece[j * three : (j + 1) * three] = turned[pl.ds(pl.multiple_of(j * part + low, 8), three), :]
        for j in range(2):
            piece[(count + j) * three : (count + j + 1) * three] = out_acc[
                pl.ds(pl.multiple_of(low, 8), three), j * halfway : (j + 1) * halfway
            ]
        outs[shift][...] = piece[...].astype(BF16)


def weight_grads(place, sent, normed, pieces, ny, after):
    heads, rows = sent.shape[2], sent.shape[4]
    width = normed[0].shape[-1]
    part = heads * HEAD
    height = (width // part + 2) * (part // ny)
    whole = lambda a: pl.BlockSpec(a.shape, lambda i: (0,) * a.ndim)
    cot_spec = pl.BlockSpec((1, rows, width), lambda i: (2, 0, 0))
    out = jax.ShapeDtypeStruct((height, 3 * PAD), BF16)
    return pl.pallas_call(
        weights_kernel,
        grid=(1,),
        in_specs=[pl.BlockSpec(memory_space=pltpu.SMEM), whole(sent)]
        + [whole(v) for v in normed]
        + [cot_spec] * len(pieces)
        + [pl.BlockSpec(memory_space=pl.ANY)] * len(after),
        out_specs=[pl.BlockSpec(out.shape, lambda i: (0, 0))] * ny,
        out_shape=[out] * ny,
        scratch_shapes=[
            pltpu.VMEM((width, 3 * PAD), F32),
            pltpu.VMEM((part, width), F32),
            pltpu.VMEM((height, 3 * PAD), F32),
        ],
        compiler_params=pltpu.CompilerParams(vmem_limit_bytes=VMEM_LIMIT),
        cost_estimate=cost(6),
        name="weight_grads",
    )(place, sent, *normed, *pieces, *after)


def attention_kernel(scale, place, *refs):
    own_refs, bias_refs, send_ref, pair_refs = refs[:4], refs[4:8], refs[-15], refs[-14:-10]
    bias, pair, kt, vt, k_all, v_all, qt, gt, dk_acc, dv_acc = refs[-10:]
    step = pl.program_id(0)
    at_x, at_zh, at_y, at_c = place[0], place[1], place[2], place[4]
    nx = len(own_refs)
    rows = own_refs[0].shape[2]
    wide = bias.shape[0] // rows
    ny = len(bias_refs)
    chunk = rows // ny
    total = kt.shape[2]
    block = wide * rows
    spots = []
    for x in range(wide):
        for shift in range(ny):
            start = x * rows + lax.rem(at_y + shift, ny) * chunk
            spots.append((x, shift, pl.ds(pl.multiple_of(start, chunk), chunk)))

    @pl.when(step == 0)
    def _():
        for ref in (kt, vt, qt, gt, dk_acc, dv_acc):
            ref[...] = jnp.zeros_like(ref)
        for t in range(2):
            for shift in range(nx):
                slot = lax.rem(at_x + shift, nx)
                own = pl.ds(pl.multiple_of((slot * 2 + at_zh) * rows, rows), rows)
                other = pl.ds(pl.multiple_of((slot * 2 + 1 - at_zh) * rows, rows), rows)
                here = pl.ds(pl.multiple_of(slot * rows, rows), rows)
                for kind, (ref, lanes) in enumerate(
                    ((qt, here), (kt, own), (vt, own), (gt, here), (kt, other), (vt, other))
                ):
                    low = kind * HEAD
                    ref[t, :HEAD, lanes] = own_refs[shift][t, low : low + HEAD, :]
            k_all[t] = kt[t].T
            v_all[t] = vt[t].T

    for x, shift, spot in spots:
        bias[spot, :] = bias_refs[shift][x]
    lanes = pl.ds(pl.multiple_of(step * block, block), block)
    for t in range(2):
        s = lax.rem(at_c + t, 2)
        q_t, g_t = qt[t, :, lanes], gt[t, :, lanes]
        scores = jnp.dot(q_t.T, kt[t], preferred_element_type=F32) * scale + bias[...].astype(F32)
        peak = jnp.max(scores, axis=-1, keepdims=True)
        expo = jnp.exp(scores - peak)
        probs = expo * (1.0 / jnp.sum(expo, axis=-1, keepdims=True))
        probs_b = probs.astype(BF16)
        att = jnp.dot(probs_b, v_all[t], preferred_element_type=F32).T
        grad_prob = jnp.dot(g_t.T, vt[t], preferred_element_type=F32)
        centre = jnp.sum(probs * grad_prob, axis=-1, keepdims=True)
        grad_score = probs * (grad_prob - centre)
        score_b = grad_score.astype(BF16)
        if t == 0:
            pair[...] = grad_score
        else:
            pair[...] += grad_score
        dq = (jnp.dot(score_b, k_all[t], preferred_element_type=F32) * scale).T
        dk_acc[t] += jnp.dot(q_t[:HEAD], score_b, preferred_element_type=F32)
        dv_acc[t] += jnp.dot(g_t[:HEAD], probs_b, preferred_element_type=F32)
        for x in range(wide):
            send_ref[step * wide + x, s, 0, :HEAD] = att[:HEAD, x * rows : (x + 1) * rows].astype(BF16)
            send_ref[step * wide + x, s, 0, HEAD : 2 * HEAD] = dq[:HEAD, x * rows : (x + 1) * rows].astype(BF16)
    for x, shift, spot in spots:
        pair_refs[shift][x] = pair[spot, :].astype(BF16)

    @pl.when(step == pl.num_programs(0) - 1)
    def _():
        for t in range(2):
            s = lax.rem(at_c + t, 2)
            for at in range(total // rows):
                x, zh = at // 2, at % 2
                low = (2 + 2 * zh) * HEAD
                part = slice(at * rows, (at + 1) * rows)
                send_ref[x, s, 0, low : low + HEAD] = (dk_acc[t, :HEAD, part] * scale).astype(BF16)
                send_ref[x, s, 0, low + HEAD : low + 2 * HEAD] = dv_acc[t, :HEAD, part].astype(BF16)


def attention(head, heads, place, own, bias, sent, scale):
    nx, chunk, total = bias[0].shape
    rows = own[0].shape[2]
    wide = 2
    block = wide * rows
    own_spec = pl.BlockSpec((2, 6 * HEAD, rows), lambda i: (0, head, 0))
    bias_spec = pl.BlockSpec((wide, chunk, total), lambda i: (i, 0, 0))
    pair_shape = jax.ShapeDtypeStruct(bias[0].shape, BF16)
    return pl.pallas_call(
        lambda *refs: attention_kernel(scale, *refs),
        grid=(nx // wide,),
        in_specs=[pl.BlockSpec(memory_space=pltpu.SMEM)]
        + [own_spec] * 4
        + [bias_spec] * 4
        + [pl.BlockSpec(memory_space=pl.ANY)] * len(sent),
        out_specs=[pl.BlockSpec((nx, 2, 1, 6 * HEAD, rows), lambda i: (0, 0, head, 0, 0))] + [bias_spec] * 4,
        out_shape=[jax.ShapeDtypeStruct((nx, 2, heads, 6 * HEAD, rows), BF16)] + [pair_shape] * 4,
        input_output_aliases={9 + i: i for i in range(len(sent))},
        scratch_shapes=[
            pltpu.VMEM((block, total), BF16),
            pltpu.VMEM((block, total), F32),
            pltpu.VMEM((2, PAD, total), BF16),
            pltpu.VMEM((2, PAD, total), BF16),
            pltpu.VMEM((2, total, PAD), BF16),
            pltpu.VMEM((2, total, PAD), BF16),
            pltpu.VMEM((2, PAD, nx * rows), BF16),
            pltpu.VMEM((2, PAD, nx * rows), BF16),
            pltpu.VMEM((2, HEAD, total), F32),
            pltpu.VMEM((2, HEAD, total), F32),
        ],
        compiler_params=pltpu.CompilerParams(vmem_limit_bytes=VMEM_LIMIT),
        cost_estimate=cost(9),
        name="attention",
    )(place, *own, *bias, *sent)


def exchange(values, axes):
    return lax.all_to_all(values, axes, split_axis=0, concat_axis=0, tiled=True)


def ring(n, shift):
    return [(i, (i + shift) % n) for i in range(n)]


def around(values, axis):
    n = lax.axis_size(axis)
    return [values] + [lax.ppermute(values, axis, ring(n, -shift)) for shift in range(1, n)]


def ring_scatter(pieces, axis):
    n = lax.axis_size(axis)
    return [lax.ppermute(pieces[shift], axis, ring(n, shift)) for shift in range(1, n)]


def added(own, got):
    total = own.astype(F32)
    for piece in got:
        total = total + piece.astype(F32)
    return total


def per_device(activations, pair_bias, w_qkv, w_out, cotangent):
    act = activations[0]
    cot = cotangent[0]
    rows, width = act.shape
    nx, nzh, ny, nzl, nc = (lax.axis_size(a) for a in AXES)
    place = jnp.stack([lax.axis_index(a) for a in AXES]).astype(jnp.int32)
    at_x, at_zh, at_c = place[0], place[1], place[4]
    groups = nx * nc
    heads = H // groups
    part = width // groups
    scale = 1.0 / math.sqrt(HEAD)
    total = pair_bias.shape[2]
    own_rows = pair_bias.shape[1]
    chunk = nzl * nc * own_rows
    swap = [(0, 1), (1, 0)]

    with jax.named_scope("rows_in"):
        act_other = lax.ppermute(act, "zh", swap)
        columns, rows_out = own_columns(place, w_qkv, w_out)
        pieces = around(jnp.stack([act, act_other, cot]), "x")
        twin = lax.ppermute(pieces[0], "c", swap)

    with jax.named_scope("project"):
        first = project(pieces[:1], [twin], columns, rows_out)

    with jax.named_scope("bias_in"):
        send = pair_bias.reshape(nx, 1, nc, heads, own_rows, total)
        send = jnp.broadcast_to(send, (nx, nzl, nc, heads, own_rows, total))
        got = exchange(send.reshape(nx * nzl * nc, heads, own_rows, total), ("x", "zl", "c"))
        got = gate(got, first[1]).reshape(nx, nzl * nc, heads, own_rows, total)
        bias = [around(got[:, :, h].reshape(nx, chunk, total), "y") for h in range(heads)]

    with jax.named_scope("project"):
        pieces = [pieces[0], pieces[1], gate(pieces[2], *bias[0][1:]), pieces[3]]
        twins = [twin] + [lax.ppermute(piece, "c", swap) for piece in pieces[1:]]
        later = project(pieces[1:], twins[1:], columns, rows_out)
        normed = first[:1] + later[: nx - 1]
        own = first[1:] + later[nx - 1 :]

    sent = []
    pairs_out = []
    with jax.named_scope("attention"):
        for h in range(heads):
            out, *pair = attention(h, heads, place, own, bias[h], sent, scale)
            sent = [out]
            pairs_out.append(pair)

    with jax.named_scope("along_y"):
        arrived = [ring_scatter(pair, "y") for pair in pairs_out]
        sums = [added(pair[0], got) for pair, got in zip(pairs_out, arrived)]
        sums = [v.astype(BF16).reshape(nx * nzl * nc, own_rows, total) for v in sums]

    with jax.named_scope("weights"):
        weight_pieces = weight_grads(place, sent[0], normed, pieces + twins, ny, arrived[0][:1])

    with jax.named_scope("along_y"):
        weight_sum = added(weight_pieces[0], ring_scatter(weight_pieces, "y")).astype(BF16)

    with jax.named_scope("owners"):
        three = width // (nx * nzh * ny * nzl * nc)
        cut = nx * nzh * nzl * nc * three
        qkv_part = weight_sum[:cut].reshape(nx, nzh, nzl, nc, three, 3 * PAD).transpose(0, 2, 3, 1, 4, 5)
        out_part = weight_sum[cut:].reshape(1, 2, nzl, nc, three, width // 2).transpose(0, 2, 3, 1, 4, 5)
        here = (jnp.arange(nx) == at_x).reshape(nx, 1, 1, 1, 1, 1)
        out_part = jnp.where(here, out_part, jnp.zeros_like(out_part))
        peers = nx * nzl * nc
        weight_send = jnp.concatenate(
            [qkv_part.reshape(peers, -1), out_part.reshape(peers, -1)], axis=1
        ).reshape(peers, heads * own_rows, -1)
        pair_send = jnp.concatenate(sums, axis=1)
        got = exchange(jnp.concatenate([pair_send, weight_send], axis=2), ("x", "zl", "c"))
        pair_got = got[:, :, :total].reshape(nx, nzl, nc, heads, own_rows, total).astype(F32)
        grad_pair = jnp.sum(pair_got, axis=1).astype(BF16).reshape(H, own_rows, total)
        weight_got = jnp.sum(got[:, :, total:].reshape(nx, nzl, nc, -1).astype(F32), axis=1)
        cut = nzh * three * 3 * PAD
        qkv_part = weight_got[:, :, :cut].reshape(groups, nzh, three, 3, PAD)[..., :part]
        qkv_part = qkv_part.transpose(1, 2, 3, 0, 4).reshape(nzh, three, 3 * width)
        out_part = jnp.sum(weight_got[:, :, cut:], axis=0).reshape(nzh, 2, three, width // 2)
        out_part = out_part.transpose(0, 2, 1, 3).reshape(nzh, three, width)
        partial = jnp.concatenate([qkv_part, out_part], axis=2)
        away = lax.dynamic_index_in_dim(partial, 1 - at_zh, 0, keepdims=False).astype(BF16)
        grad_weights = lax.dynamic_index_in_dim(partial, at_zh, 0, keepdims=False)
        grad_weights = grad_weights + lax.ppermute(away, "zh", swap).astype(F32)

    with jax.named_scope("tokens_out"):
        got = exchange(sent[0].reshape(groups, heads * 6 * HEAD, rows), ("x", "c"))
        got = got.reshape(groups, heads, 6, HEAD, rows)
        attended = got[:, :, 0].reshape(width, rows)
        grad_query = got[:, :, 1].reshape(width, rows)
        grad_kv = got[:, :, 2:].reshape(groups, heads, nzh, 2, HEAD, rows).transpose(2, 3, 0, 1, 4, 5)
        grad_kv = grad_kv.reshape(nzh, 2 * width, rows)
        kv_own = lax.dynamic_index_in_dim(grad_kv, at_zh, 0, keepdims=False)
        kv_other = lax.dynamic_index_in_dim(grad_kv, 1 - at_zh, 0, keepdims=False)

        def product(left, right, dims):
            return lax.dot_general(left, right, (dims, ((), ())), preferred_element_type=F32)

        grad_other = product(kv_other, w_qkv[:, width:], ((0,), (1,))).astype(BF16)
        grad_other = lax.ppermute(grad_other, "zh", swap)
        update = product(attended, w_out, ((0,), (0,))).astype(BF16)
        grad_own = product(jnp.concatenate([grad_query, kv_own], axis=0), w_qkv, ((0,), (1,)))
        normed, inverse = layer_norm(act.astype(F32))
        grad_act = norm_backward(grad_own + grad_other.astype(F32), normed, inverse).astype(BF16)

    return (update[None], grad_act[None], grad_pair, grad_weights)


def solution(mesh):
    fine = Mesh(mesh.devices.reshape(4, 2, 4, 4, 2), AXES)
    row, samp = ("x", "zh"), ("y", "zl", "c")
    in_specs = (
        P(samp, row, None),
        P(None, row + samp, None),
        P(),
        P(),
        P(samp, row, None),
    )
    out_specs = (
        P(samp, row, None),
        P(samp, row, None),
        P(None, row + samp, None),
        P(row + samp, None),
    )
    return jax.shard_map(
        per_device, mesh=fine, in_specs=in_specs, out_specs=out_specs, check_vma=False
    )
```
